32 devices in a mesh: dom: 2 (over y), blk: 8 (over z, core), field: 2 (over x).
Axes of the slice: x: 2, y: 2, z: 4, core: 2. Of those that a mesh axis runs over, the one named last changes fastest.
Arguments:
- stiffness: bfloat16 [256, 27, 128, 128], P(('dom', 'blk'), None, 'field'), may hold values from -3 to 3
- prolong: bfloat16 [256, 2, 4096], P(('dom', 'blk'), 'field'), may hold values from -0.75 to 0.75
- columns: int32 [256, 27], P(('dom', 'blk')), may hold values from 0 to 19
- counts: int32 [16, 16], P(('dom', 'blk')), may hold values from 1 to 27, 256 in all within a row
- aggregate: int32 [256], P(('dom', 'blk')), may hold values from 0 to 4, as said below
- coarse_slots: int32 [256, 27], P(('dom', 'blk')), may hold values from 0 to 26
- requests: int32 [16, 2, 2], P(('dom', 'blk')), may hold values from 0 to 15
Outputs:
- coarse_matrix: bfloat16 [64, 27, 128, 128], P(('dom', 'blk'), None, 'field')
The draws below stay inside these ranges and needn't reach their ends.
Inputs may be any that keep to these rules, and one draw needn't show every extreme that they name: `columns`: below 16 an entry names a row of the device itself; 16 + p * 2 + q names row q received from the device with dom index p. Each device's 16 counts sum to 256. The last fine row of every device has aggregate 4; all others lie below 4. `requests`: entry [g, p, q] is the row of device g that the device with dom index p receives in its place q.
All inputs are finite; a program needn't handle non-finite values.
Results may differ from the reference program's by a relative error of at most 0.0049.
Values may be sent and summed in bfloat16 or wider, within the bound.
No kernel may reach another device: no remote copies, remote signals or barrier semaphores. Data moves between devices by JAX's collectives and lax.ppermute only.
A program may use at most 128 MiB of HBM per device.

```python
import math
import jax
import jax.numpy as jnp
import numpy as np
from jax import lax

BS = 64
CB = 64
NK = 27
CSLOT = 27
AVGNZ = 16
Q = 2
ROWS = 16
NC_DEV = 4
GROUPS = 16
NF = 256
NCO = 64
N_DOM = 2
N_BLK = 8


def draw_aggregate(key, part):
    drawn = jax.random.randint(key, (NF,), 0, NC_DEV)
    position = jnp.arange(NF) % ROWS
    return jnp.where(position == ROWS - 1, NC_DEV, drawn).astype(jnp.int32)


def place_ends(entries, own_key, low, high):
    shape = entries.shape
    place = [jax.random.randint(jax.random.fold_in(own_key, axis), (), 0, shape[axis]) for axis in range(len(shape))]
    entries = entries.at[tuple(place)].set(low)
    longest = shape.index(max(shape))
    place[longest] = (place[longest] + 1) % shape[longest]
    return entries.at[tuple(place)].set(high)


def level_of(key, dims, cuts, low, top_value):
    gain = 1.0
    for dim, shards_of in cuts:
        draws = jax.random.uniform(jax.random.fold_in(jax.random.fold_in(key, 6), dim), (shards_of,), jnp.float32, low / len(cuts), top_value / len(cuts))
        gain = gain * jnp.repeat(jnp.exp(draws), dims[dim] // shards_of).reshape((-1,) + (1,) * (len(dims) - 1 - dim))
    return gain


def profile(number_of, total, reach, slope):
    portions = [(1 << 20) // math.isqrt(grade ** slope) + 1 for grade in range(2, number_of + 1)]
    rest, given = total - reach - (number_of - 1), [1] * (number_of - 1)
    while rest > 0:
        movable = [i for i in range(number_of - 1) if given[i] < reach]
        pool, budget = sum([portions[i] for i in movable]), rest
        for i in movable:
            addition = min(reach - given[i], max(1, budget * portions[i] // pool), rest)
            given[i] = given[i] + addition
            rest = rest - addition
    return np.array([reach] + given)


def uneven(rng, amount, total, bound, lean):
    if amount == 2:
        one = jax.random.randint(rng, (), max(1, total - bound), min(bound, total - 1) + 1)
        return jnp.stack([one, total - one])
    tallies = jnp.asarray(profile(amount, total, bound, lean), jnp.int32)
    twos = (amount - 1) // 2
    source_of, taker = tallies[1:1 + 2 * twos:2], tallies[2:2 + 2 * twos:2]
    room = jnp.minimum(source_of - 1, bound - taker)
    shifted = jax.random.randint(jax.random.fold_in(rng, 1), (twos,), 0, 1 << 20) % (room + 1)
    tallies = tallies.at[1:1 + 2 * twos:2].set(source_of - shifted).at[2:2 + 2 * twos:2].set(taker + shifted)
    return tallies[jax.random.permutation(jax.random.fold_in(rng, 2), amount)]


def centred(own_key, dims, deviation, limit, shards=(), kind=jnp.bfloat16):
    loudness = level_of(own_key, dims, shards, -0.22, 0.18) if shards else 1.0
    result = jax.random.normal(own_key, dims, jnp.float32) * deviation * loudness
    return jnp.minimum(jnp.maximum(result, -limit), limit).astype(kind)


def setup_inputs(seed: int = 0) -> dict:
    arg_keys = jax.random.split(jax.random.key(seed), 8)
    return {
        "stiffness": centred(arg_keys[0], (NF, NK, 2 * BS, 2 * BS), 0.5, 3.0, ((0, 16), (2, 2))),
        "prolong": centred(arg_keys[1], (NF, 2, BS * CB), BS ** -0.5, 0.75, ((0, 16), (1, 2))),
        "columns": place_ends(jax.random.randint(arg_keys[2], (NF, NK), 0, ROWS + N_DOM * Q), jax.random.fold_in(arg_keys[2], 1), 0, (ROWS + N_DOM * Q) - 1).astype(jnp.int32),
        "counts": jax.vmap(lambda own: uneven(own, ROWS, ROWS * AVGNZ, NK, 2))(jax.random.split(arg_keys[3], GROUPS)).reshape((GROUPS, ROWS)).astype(jnp.int32),
        "aggregate": draw_aggregate(jax.random.fold_in(arg_keys[7], 71), 0),
        "coarse_slots": place_ends(jax.random.randint(arg_keys[5], (NF, NK), 0, CSLOT), jax.random.fold_in(arg_keys[5], 1), 0, CSLOT - 1).astype(jnp.int32),
        "requests": place_ends(jax.random.randint(arg_keys[6], (GROUPS, N_DOM, Q), 0, ROWS), jax.random.fold_in(arg_keys[6], 1), 0, ROWS - 1).astype(jnp.int32),
    }


def reference(stiffness, prolong, columns, counts, aggregate, coarse_slots, requests):
    discard = (NC_DEV + 1) * CSLOT
    prolong_all = prolong.astype(jnp.float32).reshape(NF, 2, BS, CB)

    def one_group(group_index):
        dom_index = group_index // N_BLK
        blk_index = group_index % N_BLK
        first_row = group_index * ROWS
        peer_groups = jnp.arange(N_DOM, dtype=jnp.int32) * N_BLK + blk_index
        request_rows = requests[peer_groups, dom_index]
        ghost_rows = (peer_groups[:, None] * ROWS + request_rows).reshape(-1).astype(jnp.int32)
        local_rows = (first_row + jnp.arange(ROWS, dtype=jnp.int32)).astype(jnp.int32)
        extended = prolong_all[jnp.concatenate([local_rows, ghost_rows])]
        col_index = lax.dynamic_slice_in_dim(columns, first_row, ROWS, 0)
        neighbour = extended[col_index]
        stiff_rows = lax.dynamic_slice_in_dim(stiffness, first_row, ROWS, 0).astype(jnp.float32)
        stiff_rows = stiff_rows.reshape(ROWS, NK, 2, BS, 2, BS)
        applied = jnp.einsum('rkfagc,rkgcb->rkfagb', stiff_rows, neighbour).astype(jnp.bfloat16)
        applied = lax.optimization_barrier(applied).astype(jnp.float32).reshape(ROWS, NK, 2, BS, 2 * CB)
        restrict = prolong_all[local_rows]
        contrib = jnp.einsum('rfca,rkfcb->rkfab', restrict, applied)
        live_slot = jnp.arange(NK, dtype=jnp.int32)[None, :] < counts[group_index][:, None]
        agg_rows = lax.dynamic_slice_in_dim(aggregate, first_row, ROWS, 0)
        slot_rows = lax.dynamic_slice_in_dim(coarse_slots, first_row, ROWS, 0)
        target = jnp.where(live_slot, agg_rows[:, None] * CSLOT + slot_rows, discard).astype(jnp.int32)
        summed = jax.ops.segment_sum(contrib.reshape(ROWS * NK, 2, CB, 2 * CB), target.reshape(-1), num_segments=discard)
        return summed.reshape(NC_DEV + 1, CSLOT, 2, CB, 2 * CB)

    partials = lax.map(one_group, jnp.arange(GROUPS, dtype=jnp.int32))
    owned = partials[:, :NC_DEV]
    spill_rows = partials[:, NC_DEV].reshape(N_DOM, N_BLK, CSLOT, 2, CB, 2 * CB)
    arriving = jnp.roll(spill_rows, 1, axis=1).reshape(GROUPS, CSLOT, 2, CB, 2 * CB)
    owned = owned.at[:, 0].add(arriving)
    return owned.reshape(NCO, CSLOT, 2 * CB, 2 * CB).astype(jnp.bfloat16)
```

```python
import functools

import jax
import jax.numpy as jnp
from jax import lax
from jax.experimental import pallas as pl
from jax.experimental.pallas import tpu as pltpu
from jax.sharding import PartitionSpec as P

CSLOT = 27
NC_DEV = 4
UNROLL = 9

VMEM = pltpu.VMEM
SMEM = pltpu.SMEM
f32 = jnp.float32
bf16 = jnp.bfloat16


def in_vmem(x):
    return pltpu.with_memory_space_constraint(x, VMEM)


def spec(space):
    return pl.BlockSpec(memory_space=space)


def shift_pairs(n, by):
    return [(i, (i + by) % n) for i in range(n)]


def pick_kernel(n_dom, q, requests, flat, out):
    me = lax.axis_index("dom")
    rows = flat.shape[0]
    lane = lax.broadcasted_iota(jnp.int32, (1, rows), 1)
    hot = []
    for s in range(1, n_dom):
        to = lax.rem(me + s, n_dom)
        for r in range(q):
            hot.append((lane == requests[0, to, r]).astype(f32))
    hot = jnp.concatenate(hot, axis=0).astype(bf16)
    out[...] = jnp.dot(hot, flat[...], preferred_element_type=f32).astype(bf16)


def pick(requests, flat, n_dom, q):
    return pl.pallas_call(
        functools.partial(pick_kernel, n_dom, q),
        out_shape=VMEM(((n_dom - 1) * q, flat.shape[1]), bf16),
        in_specs=[spec(SMEM), spec(VMEM)],
        out_specs=spec(VMEM),
    )(requests, flat)


def entries(base, count, live, columns, slots, row, stiff, restrict, table, acc, offset, trash):
    applied = []
    for u in range(count):
        k = base + u
        j = columns[row, k]
        x = jnp.dot(stiff[k], table[j], preferred_element_type=f32)
        applied.append(x.astype(bf16))
    for u in range(0, count, 2):
        pair = applied[u : u + 2]
        x = jnp.concatenate(pair, axis=1) if len(pair) == 2 else pair[0]
        z = jnp.dot(restrict, x, preferred_element_type=f32)
        for h in range(len(pair)):
            k = base + u + h
            seg = jnp.where(k < live, offset + slots[row, k], trash)
            acc[seg] += z[:, h * 128 : h * 128 + 128]


def spill_kernel(n_dom, q, columns, counts, slots, requests, stiffness, own, other, g_own, g_other,
                 table, out, row_buf, acc, sem):
    rows, slot_count = stiffness.shape[:2]
    last = rows - 1
    copy = pltpu.make_async_copy(stiffness.at[last], row_buf, sem)
    copy.start()
    first = lax.axis_index("field") == 0
    me = lax.axis_index("dom")
    dofs = own.shape[1]

    def put(j, mine, theirs):
        zero = jnp.zeros((dofs, dofs), bf16)
        top = jnp.where(first, mine, theirs)
        bottom = jnp.where(first, theirs, mine)
        table[j] = jnp.concatenate(
            [jnp.concatenate([top, zero], axis=1), jnp.concatenate([zero, bottom], axis=1)], axis=0)

    for j in range(rows):
        put(j, own[j], other[j])
    for s in range(1, n_dom):
        source = lax.rem(me + n_dom - s, n_dom)
        for r in range(q):
            put(rows + source * q + r, g_own[(s - 1) * q + r], g_other[(s - 1) * q + r])
    for r in range(q):
        table[rows + me * q + r] = table[requests[0, me, r]]
    acc[...] = jnp.zeros_like(acc)
    copy.wait()
    live = counts[0, last]
    restrict = own[last].T
    for c in range(slot_count // UNROLL):
        @pl.when(c * UNROLL < live)
        def _():
            entries(c * UNROLL, UNROLL, live, columns, slots, last, row_buf, restrict, table, acc, 0, CSLOT)
    out[...] = acc[0:CSLOT].astype(bf16)


def main_kernel(columns, counts, aggregate, slots, stiffness, own, table, out, first_row, stiff, acc, stage, sems, out_sem):
    rows, slot_count = stiffness.shape[:2]
    last = rows - 1
    for i in range(last):
        pltpu.make_async_copy(stiffness.at[i], stiff.at[i], sems.at[i]).start()
    acc[...] = jnp.zeros_like(acc)

    @pl.loop(0, last)
    def _(i):
        pltpu.make_async_copy(stiffness.at[i], stiff.at[i], sems.at[i]).wait()
        live = counts[0, i]
        restrict = own[i].T
        offset = aggregate[i] * CSLOT

        @pl.loop(0, (live + (UNROLL - 1)) // UNROLL)
        def _(c):
            entries(c * UNROLL, UNROLL, live, columns, slots, i, stiff.at[i], restrict, table, acc,
                    offset, NC_DEV * CSLOT)

    first_row[...] = acc[0:CSLOT]
    for c in range(1, NC_DEV):
        stage[c - 1] = acc[c * CSLOT : (c + 1) * CSLOT].astype(bf16)
    copy = pltpu.make_async_copy(stage, out.at[1:NC_DEV], out_sem)
    copy.start()
    copy.wait()


def final_kernel(partial, incoming, _, out, stage, sem):
    stage[...] = (partial[...] + incoming[...].astype(f32)).astype(bf16)
    copy = pltpu.make_async_copy(stage, out.at[0], sem)
    copy.start()
    copy.wait()


def shards(stiffness, prolong, columns, counts, aggregate, coarse_slots, requests):
    rows, slot_count, dofs, width = stiffness.shape
    coarse = prolong.shape[2] // dofs
    n_dom = lax.axis_size("dom")
    n_field = lax.axis_size("field")
    q = requests.shape[2]
    own_flat = prolong[:, 0, :]
    other_flat = lax.ppermute(own_flat, "field", [(0, 1), (1, 0)])
    picked = pick(requests, own_flat, n_dom, q)
    g_own, g_other = [], []
    for s in range(1, n_dom):
        part = picked[(s - 1) * q : s * q]
        g_own.append(lax.ppermute(part, "dom", shift_pairs(n_dom, s)))
        pairs = [(d * n_field + f, ((d + s) % n_dom) * n_field + 1 - f) for d in range(n_dom) for f in range(n_field)]
        g_other.append(lax.ppermute(part, ("dom", "field"), pairs))
    g_own = jnp.concatenate(g_own, axis=0)
    g_other = jnp.concatenate(g_other, axis=0)
    as_blocks = lambda x: x.reshape(x.shape[0], dofs, coarse)
    own, other = as_blocks(own_flat), as_blocks(other_flat)
    g_own, g_other = as_blocks(g_own), as_blocks(g_other)
    n_ext = rows + n_dom * q
    limit = pltpu.CompilerParams(vmem_limit_bytes=40 * 2**20)
    table, spill = pl.pallas_call(
        functools.partial(spill_kernel, n_dom, q),
        out_shape=(VMEM((n_ext, width, 2 * coarse), bf16), VMEM((CSLOT, dofs, 2 * coarse), bf16)),
        in_specs=[spec(SMEM)] * 4 + [spec(pl.ANY)] + [spec(VMEM)] * 4,
        out_specs=(spec(VMEM), spec(VMEM)),
        scratch_shapes=[VMEM((slot_count, dofs, width), bf16), VMEM((CSLOT + 1, coarse, 2 * coarse), f32),
                        pltpu.SemaphoreType.DMA(())],
        compiler_params=limit,
        cost_estimate=pl.CostEstimate(flops=10**7, bytes_accessed=10**6, transcendentals=0),
    )(columns, counts, coarse_slots, requests, stiffness, in_vmem(own), in_vmem(other), in_vmem(g_own), in_vmem(g_other))
    incoming = lax.ppermute(spill, "blk", shift_pairs(lax.axis_size("blk"), 1))
    out_shape = jax.ShapeDtypeStruct((NC_DEV, CSLOT, coarse, 2 * coarse), bf16)
    out, partial = pl.pallas_call(
        main_kernel,
        out_shape=(out_shape, VMEM((CSLOT, coarse, 2 * coarse), f32)),
        in_specs=[spec(SMEM)] * 4 + [spec(pl.ANY)] + [spec(VMEM)] * 2,
        out_specs=(spec(pl.ANY), spec(VMEM)),
        scratch_shapes=[VMEM((rows, slot_count, dofs, width), bf16),
                        VMEM((NC_DEV * CSLOT + 1, coarse, 2 * coarse), f32),
                        VMEM((NC_DEV - 1, CSLOT, coarse, 2 * coarse), bf16),
                        pltpu.SemaphoreType.DMA((rows,)), pltpu.SemaphoreType.DMA(())],
        compiler_params=limit,
        cost_estimate=pl.CostEstimate(flops=10**9, bytes_accessed=10**7, transcendentals=0),
    )(columns, counts, aggregate, coarse_slots, stiffness, in_vmem(own), in_vmem(table))
    return pl.pallas_call(
        final_kernel,
        out_shape=out_shape,
        in_specs=[spec(VMEM), spec(VMEM), spec(pl.ANY)],
        out_specs=spec(pl.ANY),
        scratch_shapes=[VMEM((CSLOT, coarse, 2 * coarse), bf16), pltpu.SemaphoreType.DMA(())],
        input_output_aliases={2: 0},
        compiler_params=limit,
    )(in_vmem(partial), in_vmem(incoming), out)


def solution(mesh):
    in_specs = (
        P(("dom", "blk"), None, "field", None),
        P(("dom", "blk"), "field", None),
        P(("dom", "blk"), None),
        P(("dom", "blk"), None),
        P(("dom", "blk")),
        P(("dom", "blk"), None),
        P(("dom", "blk"), None, None),
    )
    out_specs = P(("dom", "blk"), None, "field", None)
    return jax.shard_map(shards, mesh=mesh, in_specs=in_specs, out_specs=out_specs, check_vma=False)
```

```python
import functools

import jax
import jax.numpy as jnp
from jax import lax
from jax.experimental import pallas as pl
from jax.experimental.pallas import tpu as pltpu
from jax.sharding import PartitionSpec as P

CSLOT = 27
NC_DEV = 4
AVGNZ = 16
UNROLL = 32
COLUMN_BIT = 10
SEG_BIT = 16

VMEM = pltpu.VMEM
SMEM = pltpu.SMEM
f32 = jnp.float32
bf16 = jnp.bfloat16


def in_vmem(x):
    return pltpu.with_memory_space_constraint(x, VMEM)


def in_hbm(x):
    return pltpu.with_memory_space_constraint(x, pltpu.HBM)


def spec(space):
    return pl.BlockSpec(memory_space=space)


def shift_pairs(n, by):
    return [(i, (i + by) % n) for i in range(n)]


def pick_kernel(n_dom, q, requests, flat, out):
    me = lax.axis_index("dom")
    rows = flat.shape[0]
    lane = lax.broadcasted_iota(jnp.int32, (1, rows), 1)
    hot = []
    for s in range(1, n_dom):
        to = lax.rem(me + s, n_dom)
        for r in range(q):
            hot.append((lane == requests[0, to, r]).astype(f32))
    hot = jnp.concatenate(hot, axis=0).astype(bf16)
    out[...] = jnp.dot(hot, flat[...], preferred_element_type=f32).astype(bf16)


def pick(requests, flat, n_dom, q):
    return pl.pallas_call(
        functools.partial(pick_kernel, n_dom, q),
        out_shape=VMEM(((n_dom - 1) * q, flat.shape[1]), bf16),
        in_specs=[spec(SMEM), spec(VMEM)],
        out_specs=spec(VMEM),
    )(requests, flat)


def list_kernel(columns, counts, aggregate, slots, out, packed_v, packed, sem):
    rows, slot_count = columns.shape
    block = lax.broadcasted_iota(jnp.int32, (rows, slot_count), 0) * slot_count
    block = block + lax.broadcasted_iota(jnp.int32, (rows, slot_count), 1)
    packed_v[0:rows, 0:slot_count] = block + (columns[...] << COLUMN_BIT) + (slots[...] << SEG_BIT)
    copy = pltpu.make_async_copy(packed_v, packed, sem)
    copy.start()
    copy.wait()
    base = 0
    for i in range(rows - 1):
        offset = (aggregate[i] * CSLOT) << SEG_BIT
        for k in range(slot_count):
            out[base + k] = packed[i, k] + offset
        base = base + counts[0, i]
    for k in range(slot_count):
        out[base + k] = (NC_DEV * CSLOT) << SEG_BIT


def table_of(n_dom, q, requests, own, other, g_own, g_other, table):
    rows, dofs = own.shape[:2]
    first = lax.axis_index("field") == 0
    me = lax.axis_index("dom")

    def put(j, mine, theirs):
        zero = jnp.zeros((dofs, dofs), bf16)
        top = jnp.where(first, mine, theirs)
        bottom = jnp.where(first, theirs, mine)
        table[j] = jnp.concatenate(
            [jnp.concatenate([top, zero], axis=1), jnp.concatenate([zero, bottom], axis=1)], axis=0)

    for j in range(rows):
        put(j, own[j], other[j])
    for s in range(1, n_dom):
        source = lax.rem(me + n_dom - s, n_dom)
        for r in range(q):
            put(rows + source * q + r, g_own[(s - 1) * q + r], g_other[(s - 1) * q + r])
    for r in range(q):
        table[rows + me * q + r] = table[requests[0, me, r]]


def spill_kernel(n_dom, q, columns, counts, slots, requests, stiffness, own, other, g_own, g_other,
                 table, out, row_buf, acc, sem):
    rows, slot_count = stiffness.shape[:2]
    last = rows - 1
    copy = pltpu.make_async_copy(stiffness.at[last], row_buf, sem)
    copy.start()
    table_of(n_dom, q, requests, own, other, g_own, g_other, table)
    acc[...] = jnp.zeros_like(acc)
    live = counts[0, last]
    restrict = own[last].T
    copy.wait()
    applied = [
        jnp.dot(row_buf[k], table[columns[last, k]], preferred_element_type=f32).astype(bf16) for k in range(slot_count)
    ]
    products = [jnp.dot(restrict, x, preferred_element_type=f32) for x in applied]
    for k in range(slot_count):
        acc[jnp.where(k < live, slots[last, k], CSLOT)] += products[k]
    out[...] = acc[0:CSLOT].astype(bf16)


def main_kernel(listed, stiffness, own, table, out, first_row, stiff, restrict, acc, stage, sems, out_sem):
    rows, slot_count = stiffness.shape[:2]
    for i in range(rows - 1):
        pltpu.make_async_copy(stiffness.at[i], stiff.at[pl.ds(i * slot_count, slot_count)], sems.at[i]).start()
    acc[...] = jnp.zeros_like(acc)
    for i in range(rows):
        restrict[i] = own[i].T

    def chunk(c, arrived):
        words = [listed[c * UNROLL + u] for u in range(UNROLL)]
        blocks = [w & (2**COLUMN_BIT - 1) for w in words]
        needed = blocks[UNROLL - 1] // slot_count + 1
        needed = jnp.where(c == chunks - 1, rows - 1, needed)

        @pl.loop(arrived, needed)
        def _(i):
            pltpu.make_async_copy(stiffness.at[i], stiff.at[pl.ds(i * slot_count, slot_count)], sems.at[i]).wait()

        applied = [
            jnp.dot(stiff[b], table[(w >> COLUMN_BIT) & (2 ** (SEG_BIT - COLUMN_BIT) - 1)],
                    preferred_element_type=f32).astype(bf16) for w, b in zip(words, blocks)
        ]
        products = [jnp.dot(restrict[b // slot_count], x, preferred_element_type=f32) for b, x in zip(blocks, applied)]
        for w, z in zip(words, products):
            acc[w >> SEG_BIT] += z
        return jnp.maximum(arrived, needed)

    chunks = (rows * AVGNZ) // UNROLL
    lax.fori_loop(0, chunks, chunk, 0)
    first_row[...] = acc[0:CSLOT]
    for c in range(1, NC_DEV):
        stage[c - 1] = acc[c * CSLOT : (c + 1) * CSLOT].astype(bf16)
    copy = pltpu.make_async_copy(stage, out.at[1:NC_DEV], out_sem)
    copy.start()
    copy.wait()


def final_kernel(partial, incoming, _, out, stage, sem):
    stage[...] = (partial[...] + incoming[...].astype(f32)).astype(bf16)
    copy = pltpu.make_async_copy(stage, out.at[0], sem)
    copy.start()
    copy.wait()


def shards(stiffness, prolong, columns, counts, aggregate, coarse_slots, requests):
    rows, slot_count, dofs, width = stiffness.shape
    coarse = prolong.shape[2] // dofs
    n_dom = lax.axis_size("dom")
    n_field = lax.axis_size("field")
    q = requests.shape[2]
    own_flat = prolong[:, 0, :]
    other_flat = lax.ppermute(own_flat, "field", [(0, 1), (1, 0)])
    picked = pick(requests, own_flat, n_dom, q)
    g_own, g_other = [], []
    for s in range(1, n_dom):
        part = picked[(s - 1) * q : s * q]
        g_own.append(lax.ppermute(part, "dom", shift_pairs(n_dom, s)))
        pairs = [(d * n_field + f, ((d + s) % n_dom) * n_field + 1 - f) for d in range(n_dom) for f in range(n_field)]
        g_other.append(lax.ppermute(part, ("dom", "field"), pairs))
    g_own = jnp.concatenate(g_own, axis=0)
    g_other = jnp.concatenate(g_other, axis=0)
    as_blocks = lambda x: x.reshape(x.shape[0], dofs, coarse)
    own, other = as_blocks(own_flat), as_blocks(other_flat)
    g_own, g_other = as_blocks(g_own), as_blocks(g_other)
    n_ext = rows + n_dom * q
    limit = pltpu.CompilerParams(vmem_limit_bytes=40 * 2**20)
    columns, counts, aggregate, coarse_slots, requests, stiffness = map(
        in_hbm, (columns, counts, aggregate, coarse_slots, requests, stiffness))
    table, spill = pl.pallas_call(
        functools.partial(spill_kernel, n_dom, q),
        out_shape=(VMEM((n_ext, width, 2 * coarse), bf16), VMEM((CSLOT, dofs, 2 * coarse), bf16)),
        in_specs=[spec(SMEM)] * 4 + [spec(pl.ANY)] + [spec(VMEM)] * 4,
        out_specs=(spec(VMEM), spec(VMEM)),
        scratch_shapes=[VMEM((slot_count, dofs, width), bf16), VMEM((CSLOT + 1, coarse, 2 * coarse), f32),
                        pltpu.SemaphoreType.DMA(())],
        compiler_params=limit,
        cost_estimate=pl.CostEstimate(flops=10**7, bytes_accessed=10**6, transcendentals=0),
    )(columns, counts, coarse_slots, requests, stiffness, in_vmem(own), in_vmem(other), in_vmem(g_own), in_vmem(g_other))
    incoming = lax.ppermute(spill, "blk", shift_pairs(lax.axis_size("blk"), 1))
    listed = pl.pallas_call(
        list_kernel,
        out_shape=jax.ShapeDtypeStruct((rows * AVGNZ + 2 * slot_count,), jnp.int32),
        in_specs=[spec(VMEM), spec(SMEM), spec(SMEM), spec(VMEM)],
        out_specs=spec(SMEM),
        scratch_shapes=[VMEM((rows, 128), jnp.int32), SMEM((rows, 128), jnp.int32), pltpu.SemaphoreType.DMA(())],
    )(columns, counts, aggregate, coarse_slots)
    out_shape = jax.ShapeDtypeStruct((NC_DEV, CSLOT, coarse, 2 * coarse), bf16)
    out, partial = pl.pallas_call(
        main_kernel,
        out_shape=(out_shape, VMEM((CSLOT, coarse, 2 * coarse), f32)),
        in_specs=[spec(SMEM), spec(pl.ANY)] + [spec(VMEM)] * 2,
        out_specs=(spec(pl.ANY), spec(VMEM)),
        scratch_shapes=[VMEM((rows * slot_count, dofs, width), bf16), VMEM((rows, coarse, dofs), bf16),
                        VMEM((NC_DEV * CSLOT + 1, coarse, 2 * coarse), f32),
                        VMEM((NC_DEV - 1, CSLOT, coarse, 2 * coarse), bf16),
                        pltpu.SemaphoreType.DMA((rows,)), pltpu.SemaphoreType.DMA(())],
        compiler_params=limit,
        cost_estimate=pl.CostEstimate(flops=10**9, bytes_accessed=10**7, transcendentals=0),
    )(listed, stiffness, in_vmem(own), in_vmem(table))
    return pl.pallas_call(
        final_kernel,
        out_shape=out_shape,
        in_specs=[spec(VMEM), spec(VMEM), spec(pl.ANY)],
        out_specs=spec(pl.ANY),
        scratch_shapes=[VMEM((CSLOT, coarse, 2 * coarse), bf16), pltpu.SemaphoreType.DMA(())],
        input_output_aliases={2: 0},
        compiler_params=limit,
    )(in_vmem(partial), in_vmem(incoming), out)


def solution(mesh):
    in_specs = (
        P(("dom", "blk"), None, "field", None),
        P(("dom", "blk"), "field", None),
        P(("dom", "blk"), None),
        P(("dom", "blk"), None),
        P(("dom", "blk")),
        P(("dom", "blk"), None),
        P(("dom", "blk"), None, None),
    )
    out_specs = P(("dom", "blk"), None, "field", None)
    return jax.shard_map(shards, mesh=mesh, in_specs=in_specs, out_specs=out_specs, check_vma=False)
```

```python
import functools

import jax
import jax.numpy as jnp
from jax import lax
from jax.experimental import pallas as pl
from jax.experimental.pallas import tpu as pltpu
from jax.sharding import PartitionSpec as P

CSLOT = 27
NC_DEV = 4
AVGNZ = 16
UNROLL = 32
COLUMN_BIT = 10
SEG_BIT = 16

VMEM = pltpu.VMEM
SMEM = pltpu.SMEM
f32 = jnp.float32
bf16 = jnp.bfloat16


def in_vmem(x):
    return pltpu.with_memory_space_constraint(x, VMEM)


def in_hbm(x):
    return pltpu.with_memory_space_constraint(x, pltpu.HBM)


def spec(space):
    return pl.BlockSpec(memory_space=space)


def shift_pairs(n, by):
    return [(i, (i + by) % n) for i in range(n)]


def prepare_kernel(n_dom, q, requests, flat, columns, slots, counts, aggregate, requests_v, picked, copied, words):
    me = lax.axis_index("dom")
    rows, slot_count = columns.shape
    lane = lax.broadcasted_iota(jnp.int32, (1, rows), 1)
    hot = []
    for s in range(1, n_dom):
        to = lax.rem(me + s, n_dom)
        for r in range(q):
            hot.append((lane == requests[0, to, r]).astype(f32))
    hot = jnp.concatenate(hot, axis=0).astype(bf16)
    own = flat[...]
    picked[...] = jnp.dot(hot, own, preferred_element_type=f32).astype(bf16)
    copied[...] = own
    block = lax.broadcasted_iota(jnp.int32, (rows, slot_count), 0) * slot_count
    block = block + lax.broadcasted_iota(jnp.int32, (rows, slot_count), 1)
    words[0:rows, 0:slot_count] = block + (columns[...] << COLUMN_BIT) + (slots[...] << SEG_BIT)
    words[rows : rows + 1, 0:rows] = counts[...]
    words[rows + 1 : rows + 2, 0:rows] = aggregate[...]
    words[rows + 2 : rows + 2 + n_dom, 0:q] = requests_v[0]


def table_of(n_dom, q, words, own, other, g_own, g_other, table):
    rows, dofs = own.shape[:2]
    first = lax.axis_index("field") == 0
    me = lax.axis_index("dom")

    def put(j, mine, theirs):
        zero = jnp.zeros((dofs, dofs), bf16)
        top = jnp.where(first, mine, theirs)
        bottom = jnp.where(first, theirs, mine)
        table[j] = jnp.concatenate(
            [jnp.concatenate([top, zero], axis=1), jnp.concatenate([zero, bottom], axis=1)], axis=0)

    for j in range(rows):
        put(j, own[j], other[j])
    for s in range(1, n_dom):
        source = lax.rem(me + n_dom - s, n_dom)
        for r in range(q):
            put(rows + source * q + r, g_own[(s - 1) * q + r], g_other[(s - 1) * q + r])
    for r in range(q):
        table[rows + me * q + r] = table[words[rows + 2 + me, r]]


def block_of(word):
    return word & (2**COLUMN_BIT - 1)


def column_of(word):
    return (word >> COLUMN_BIT) & (2 ** (SEG_BIT - COLUMN_BIT) - 1)


def spill_kernel(n_dom, q, words, stiffness, own, other, g_own, g_other, table, out, row_buf, acc, sem):
    rows, slot_count = stiffness.shape[:2]
    last = rows - 1
    copy = pltpu.make_async_copy(stiffness.at[last], row_buf, sem)
    copy.start()
    table_of(n_dom, q, words, own, other, g_own, g_other, table)
    acc[...] = jnp.zeros_like(acc)
    live = words[rows, last]
    restrict = own[last].T
    copy.wait()
    listed = [words[last, k] for k in range(slot_count)]
    applied = [
        jnp.dot(row_buf[k], table[column_of(listed[k])], preferred_element_type=f32).astype(bf16)
        for k in range(slot_count)
    ]
    products = [jnp.dot(restrict, x, preferred_element_type=f32) for x in applied]
    for k in range(slot_count):
        acc[jnp.where(k < live, listed[k] >> SEG_BIT, CSLOT)] += products[k]
    out[...] = acc[0:CSLOT].astype(bf16)


def main_kernel(words, stiffness, own, table, out, first_row, listed, stiff, restrict, acc, stage, sems, out_sems):
    rows, slot_count = stiffness.shape[:2]
    for i in range(rows - 1):
        pltpu.make_async_copy(stiffness.at[i], stiff.at[pl.ds(i * slot_count, slot_count)], sems.at[i]).start()
    acc[...] = jnp.zeros_like(acc)
    base = 0
    for i in range(rows - 1):
        offset = (words[rows + 1, i] * CSLOT) << SEG_BIT
        for k in range(slot_count):
            listed[base + k] = words[i, k] + offset
        base = base + words[rows, i]
    for k in range(slot_count):
        listed[base + k] = (NC_DEV * CSLOT) << SEG_BIT
    for i in range(rows):
        restrict[i] = own[i].T

    def chunk(c, arrived):
        taken = [listed[c * UNROLL + u] for u in range(UNROLL)]
        blocks = [block_of(w) for w in taken]
        needed = blocks[UNROLL - 1] // slot_count + 1
        needed = jnp.where(c == chunks - 1, rows - 1, needed)

        @pl.loop(arrived, needed)
        def _(i):
            pltpu.make_async_copy(stiffness.at[i], stiff.at[pl.ds(i * slot_count, slot_count)], sems.at[i]).wait()

        applied = [
            jnp.dot(stiff[b], table[column_of(w)], preferred_element_type=f32).astype(bf16)
            for w, b in zip(taken, blocks)
        ]
        products = [jnp.dot(restrict[b // slot_count], x, preferred_element_type=f32) for b, x in zip(blocks, applied)]
        for w, z in zip(taken, products):
            acc[w >> SEG_BIT] += z
        return jnp.maximum(arrived, needed)

    chunks = (rows * AVGNZ) // UNROLL
    lax.fori_loop(0, chunks, chunk, 0)
    copies = [pltpu.make_async_copy(stage.at[c - 1], out.at[c], out_sems.at[c - 1]) for c in range(1, NC_DEV)]
    for c in range(1, NC_DEV):
        stage[c - 1] = acc[c * CSLOT : (c + 1) * CSLOT].astype(bf16)
        copies[c - 1].start()
    first_row[...] = acc[0:CSLOT]
    for copy in copies:
        copy.wait()


def final_kernel(partial, incoming, _, out, stage, sems):
    parts = sems.shape[0]
    size = CSLOT // parts
    copies = [pltpu.make_async_copy(stage.at[pl.ds(p * size, size)], out.at[0, pl.ds(p * size, size)], sems.at[p])
              for p in range(parts)]
    for p in range(parts):
        part = pl.ds(p * size, size)
        stage[part] = (partial[part] + incoming[part].astype(f32)).astype(bf16)
        copies[p].start()
    for copy in copies:
        copy.wait()


def shards(stiffness, prolong, columns, counts, aggregate, coarse_slots, requests):
    rows, slot_count, dofs, width = stiffness.shape
    coarse = prolong.shape[2] // dofs
    n_dom = lax.axis_size("dom")
    n_field = lax.axis_size("field")
    q = requests.shape[2]
    n_ext = rows + n_dom * q
    block_shape = (coarse, 2 * coarse)
    limit = pltpu.CompilerParams(vmem_limit_bytes=40 * 2**20)
    own_flat = prolong[:, 0, :]
    other_flat = lax.ppermute(own_flat, "field", [(0, 1), (1, 0)])
    stiffness = in_hbm(stiffness)
    picked, own_copy, words = pl.pallas_call(
        functools.partial(prepare_kernel, n_dom, q),
        out_shape=(VMEM(((n_dom - 1) * q, own_flat.shape[1]), bf16), VMEM(own_flat.shape, bf16),
                   VMEM((-(-(rows + 2 + n_dom) // 8) * 8, 128), jnp.int32)),
        in_specs=[spec(SMEM)] + [spec(VMEM)] * 6,
        out_specs=(spec(VMEM),) * 3,
    )(*map(in_hbm, (requests, own_flat, columns, coarse_slots, counts, aggregate[None], requests)))
    g_own, g_other = [], []
    for s in range(1, n_dom):
        part = picked[(s - 1) * q : s * q]
        g_own.append(lax.ppermute(part, "dom", shift_pairs(n_dom, s)))
        pairs = [(d * n_field + f, ((d + s) % n_dom) * n_field + 1 - f) for d in range(n_dom) for f in range(n_field)]
        g_other.append(lax.ppermute(part, ("dom", "field"), pairs))
    g_own = jnp.concatenate(g_own, axis=0)
    g_other = jnp.concatenate(g_other, axis=0)
    as_blocks = lambda x: in_vmem(x.reshape(x.shape[0], dofs, coarse))
    own, other = as_blocks(own_copy), as_blocks(other_flat)
    g_own, g_other = as_blocks(g_own), as_blocks(g_other)
    words = in_vmem(words)
    table, spill = pl.pallas_call(
        functools.partial(spill_kernel, n_dom, q),
        out_shape=(VMEM((n_ext, width, 2 * coarse), bf16), VMEM((CSLOT, *block_shape), bf16)),
        in_specs=[spec(SMEM), spec(pl.ANY)] + [spec(VMEM)] * 4,
        out_specs=(spec(VMEM), spec(VMEM)),
        scratch_shapes=[VMEM((slot_count, dofs, width), bf16), VMEM((CSLOT + 1, *block_shape), f32),
                        pltpu.SemaphoreType.DMA(())],
        compiler_params=limit,
        cost_estimate=pl.CostEstimate(flops=10**7, bytes_accessed=10**6, transcendentals=0),
    )(words, stiffness, own, other, g_own, g_other)
    incoming = lax.ppermute(spill, "blk", shift_pairs(lax.axis_size("blk"), 1))
    out_shape = jax.ShapeDtypeStruct((NC_DEV, CSLOT, *block_shape), bf16)
    out, partial = pl.pallas_call(
        main_kernel,
        out_shape=(out_shape, VMEM((CSLOT, *block_shape), f32)),
        in_specs=[spec(SMEM), spec(pl.ANY)] + [spec(VMEM)] * 2,
        out_specs=(spec(pl.ANY), spec(VMEM)),
        scratch_shapes=[SMEM((rows * AVGNZ + 2 * slot_count,), jnp.int32),
                        VMEM((rows * slot_count, dofs, width), bf16), VMEM((rows, coarse, dofs), bf16),
                        VMEM((NC_DEV * CSLOT + 1, *block_shape), f32),
                        VMEM((NC_DEV - 1, CSLOT, *block_shape), bf16),
                        pltpu.SemaphoreType.DMA((rows,)), pltpu.SemaphoreType.DMA((NC_DEV - 1,))],
        compiler_params=limit,
        cost_estimate=pl.CostEstimate(flops=10**9, bytes_accessed=10**7, transcendentals=0),
    )(words, stiffness, own, in_vmem(table))
    return pl.pallas_call(
        final_kernel,
        out_shape=out_shape,
        in_specs=[spec(VMEM), spec(VMEM), spec(pl.ANY)],
        out_specs=spec(pl.ANY),
        scratch_shapes=[VMEM((CSLOT, *block_shape), bf16), pltpu.SemaphoreType.DMA((3,))],
        input_output_aliases={2: 0},
        compiler_params=limit,
    )(in_vmem(partial), in_vmem(incoming), out)


def solution(mesh):
    in_specs = (
        P(("dom", "blk"), None, "field", None),
        P(("dom", "blk"), "field", None),
        P(("dom", "blk"), None),
        P(("dom", "blk"), None),
        P(("dom", "blk")),
        P(("dom", "blk"), None),
        P(("dom", "blk"), None, None),
    )
    out_specs = P(("dom", "blk"), None, "field", None)
    return jax.shard_map(shards, mesh=mesh, in_specs=in_specs, out_specs=out_specs, check_vma=False)
```

```python
import functools

import jax
import jax.numpy as jnp
from jax import lax
from jax.experimental import pallas as pl
from jax.experimental.pallas import tpu as pltpu
from jax.sharding import PartitionSpec as P

CSLOT = 27
NC_DEV = 4
HALF = 14
AVGNZ = 16
UNROLL = 32
EARLY = 2
COLUMN_BIT = 10
SEG_BIT = 16
UNUSED = NC_DEV * CSLOT

VMEM = pltpu.VMEM
SMEM = pltpu.SMEM
f32 = jnp.float32
bf16 = jnp.bfloat16


def in_vmem(x):
    return pltpu.with_memory_space_constraint(x, VMEM)


def in_hbm(x):
    return pltpu.with_memory_space_constraint(x, pltpu.HBM)


def spec(space):
    return pl.BlockSpec(memory_space=space)


def shift_pairs(n, by):
    return [(i, (i + by) % n) for i in range(n)]


def prepare_kernel(n_dom, q, flat, columns, slots, counts, aggregate, requests, stiffness, picked, copied, words,
                   last_row, columns_v, slots_v, counts_v, aggregate_v, requests_v, sems):
    rows, slot_count = columns.shape
    pairs = ((flat, copied), (requests, requests_v), (columns, columns_v), (slots, slots_v), (counts, counts_v),
             (aggregate, aggregate_v), (stiffness.at[rows - 1], last_row))
    copies = [pltpu.make_async_copy(source, target, sems.at[i]) for i, (source, target) in enumerate(pairs)]
    for copy in copies:
        copy.start()
    me = lax.axis_index("dom")
    lane = lax.broadcasted_iota(jnp.int32, (1, rows), 1)
    block = lax.broadcasted_iota(jnp.int32, (rows, slot_count), 0) * slot_count
    block = block + lax.broadcasted_iota(jnp.int32, (rows, slot_count), 1)
    copies[0].wait()
    copies[1].wait()
    hot = []
    for s in range(1, n_dom):
        to = lax.rem(me + s, n_dom)
        asked = requests_v[0, pl.ds(to, 1), :]
        for r in range(q):
            hot.append((lane == asked[:, r : r + 1]).astype(f32))
    hot = jnp.concatenate(hot, axis=0).astype(bf16)
    picked[...] = jnp.dot(hot, copied[...], preferred_element_type=f32).astype(bf16)
    for copy in copies[2:6]:
        copy.wait()
    words[0:rows, 0:slot_count] = block + (columns_v[...] << COLUMN_BIT) + (slots_v[...] << SEG_BIT)
    words[rows : rows + 1, 0:rows] = counts_v[...]
    words[rows + 1 : rows + 2, 0:rows] = aggregate_v[...]
    words[rows + 2 : rows + 2 + n_dom, 0:q] = requests_v[0]
    copies[6].wait()


def block_of(word):
    return word & (2**COLUMN_BIT - 1)


def column_of(word):
    return (word >> COLUMN_BIT) & (2 ** (SEG_BIT - COLUMN_BIT) - 1)


def early_kernel(words_v, last_row, own, stiffness, words, restricted, restricted_early, row_buf, sem, sems):
    slot_count = last_row.shape[0]
    copy = pltpu.make_async_copy(words_v, words, sem)
    copy.start()
    rows = [pltpu.make_async_copy(stiffness.at[i], row_buf.at[i], sems.at[i]) for i in range(EARLY)]
    for row in rows:
        row.start()
    restrict = own[own.shape[0] - 1].T
    for k in range(slot_count):
        restricted[k] = jnp.dot(restrict, last_row[k], preferred_element_type=f32).astype(bf16)
    copy.wait()
    for i in range(EARLY):
        restrict = own[i].T
        rows[i].wait()
        for k in range(slot_count):
            y = jnp.dot(restrict, row_buf[i, k], preferred_element_type=f32)
            restricted_early[i * slot_count + k] = y.astype(bf16)


def unfold(flat, tiles, lines, dofs):
    count, size = flat.shape
    wide = flat[...].astype(f32)
    for t in range(size // 128):
        tiles[t * count : (t + 1) * count] = wide[:, t * 128 : (t + 1) * 128]
    blocks = []
    for r in range(count):
        pairs = tiles[pl.ds(r, dofs // 2, stride=count)]
        lines[pl.ds(0, dofs // 2, stride=2)] = pairs
        lines[pl.ds(1, dofs // 2, stride=2)] = pltpu.roll(pairs, 64, 1)
        blocks.append(lines[:, 0:64].astype(bf16))
    return blocks


def lane_half():
    return lax.broadcasted_iota(jnp.int32, (64, 128), 1) < 64


def corner(field, dofs, value):
    zero = jnp.zeros_like(value)
    left = jnp.concatenate([value, zero], axis=1)
    right = jnp.concatenate([zero, value], axis=1)
    return pl.multiple_of(field * dofs, dofs), jnp.where(field == 0, left, right)


def fill_table(n_dom, q, field, words, blocks, ghosts, table, tiles, lines):
    rows, dofs = blocks.shape[:2]
    me = lax.axis_index("dom")

    def put(j, value):
        start, lines = corner(field, dofs, value)
        table[j, pl.ds(start, dofs)] = lines

    for j in range(rows):
        put(j, blocks[j])
    ghosts = unfold(ghosts, tiles, lines, dofs)
    for s in range(1, n_dom):
        source = lax.rem(me + n_dom - s, n_dom)
        for r in range(q):
            put(rows + source * q + r, ghosts[(s - 1) * q + r])
    for r in range(q):
        put(rows + me * q + r, blocks[words[rows + 2 + me, r]])


def spill_half(rows, field, words, restricted, table, out, acc):
    slot_count = restricted.shape[0]
    last = rows - 1
    acc[...] = jnp.zeros_like(acc)
    live = words[rows, last]
    listed = [words[last, k] for k in range(slot_count)]
    products = [
        jnp.dot(restricted[k], table[column_of(listed[k])], preferred_element_type=f32) for k in range(slot_count)
    ]
    for k in range(slot_count):
        acc[jnp.where(k < live, listed[k] >> SEG_BIT, CSLOT)] += products[k]
    keep = lane_half() == (field == 0)
    for s in range(HALF):
        block = acc[s]
        if s + HALF < CSLOT:
            block = jnp.where(keep, block, pltpu.roll(acc[s + HALF], 64, 1))
        out[s] = block.astype(bf16)


def own_spill_kernel(n_dom, q, words, restricted, own, ghosts, table, out, acc, tiles, lines):
    field = lax.axis_index("field")
    table[...] = jnp.zeros_like(table)
    fill_table(n_dom, q, field, words, own, ghosts, table, tiles, lines)
    spill_half(own.shape[0], field, words, restricted, table, out, acc)


def other_spill_kernel(n_dom, q, words, restricted, other, ghosts, _, table, out, acc, tiles, lines):
    field = 1 - lax.axis_index("field")
    fill_table(n_dom, q, field, words, other, ghosts, table, tiles, lines)
    spill_half(other.shape[0], field, words, restricted, table, out, acc)


def fill_list(words, listed, rows, slot_count, lead):
    base = 0
    for i in range(rows - 1):
        if i == EARLY:
            for k in range(UNROLL):
                listed[base + k] = UNUSED << SEG_BIT
            first_length = base
            base = lead
        offset = (words[rows + 1, i] * CSLOT) << SEG_BIT
        for k in range(slot_count):
            listed[base + k] = words[i, k] + offset
        base = base + words[rows, i]
    for k in range(UNROLL):
        listed[base + k] = (UNUSED << SEG_BIT) + (rows - 2) * slot_count
    return first_length, base - lead


def main_kernel(lead, words, stiffness, own, restricted_early, table, later_rows, first_row, listed, stiff, restrict, acc,
                sems):
    rows, slot_count = stiffness.shape[:2]

    def row_copy(i):
        part = pl.ds((i - EARLY) * slot_count, slot_count)
        return pltpu.make_async_copy(stiffness.at[i], stiff.at[part], sems.at[i])

    for i in range(EARLY, rows - 1):
        row_copy(i).start()
    first_length, second_length = fill_list(words, listed, rows, slot_count, lead)
    for i in range(EARLY, rows - 1):
        restrict[i] = own[i].T
    acc[...] = jnp.zeros_like(acc)

    def add(taken, restricted):
        products = [jnp.dot(y, table[column_of(w)], preferred_element_type=f32) for w, y in zip(taken, restricted)]
        for w, z in zip(taken, products):
            acc[w >> SEG_BIT] += z

    @pl.loop(0, (first_length + UNROLL - 1) // UNROLL)
    def _(c):
        taken = [listed[c * UNROLL + u] for u in range(UNROLL)]
        add(taken, [restricted_early[block_of(w)] for w in taken])

    def chunk(c, arrived):
        taken = [listed[lead + c * UNROLL + u] for u in range(UNROLL)]
        blocks = [block_of(w) for w in taken]
        needed = blocks[UNROLL - 1] // slot_count + 1

        @pl.loop(arrived, needed)
        def _(i):
            row_copy(i).wait()

        add(taken, [
            jnp.dot(restrict[b // slot_count], stiff[b - EARLY * slot_count], preferred_element_type=f32).astype(bf16)
            for b in blocks
        ])
        return needed

    lax.fori_loop(0, (second_length + UNROLL - 1) // UNROLL, chunk, EARLY)
    for c in range(1, NC_DEV):
        later_rows[c - 1] = acc[c * CSLOT : (c + 1) * CSLOT].astype(bf16)
    first_row[...] = acc[0:CSLOT]


def final_kernel(partial, own_part, other_part, later_rows, out, stage, sems):
    keep = lane_half() == (lax.axis_index("field") == 0)
    later = [pltpu.make_async_copy(later_rows.at[c - 1], out.at[c], sems.at[c]) for c in range(1, NC_DEV)]
    for copy in later:
        copy.start()
    copies = [pltpu.make_async_copy(stage.at[pl.ds(s, n)], out.at[0, pl.ds(s, n)], sem)
              for s, n, sem in ((0, HALF, sems.at[0]), (HALF, CSLOT - HALF, sems.at[NC_DEV]))]
    for s in range(HALF):
        mine, theirs = own_part[s].astype(f32), other_part[s].astype(f32)
        stage[s] = (partial[s] + jnp.where(keep, mine, theirs)).astype(bf16)
    copies[0].start()
    for s in range(HALF, CSLOT):
        mine, theirs = own_part[s - HALF].astype(f32), other_part[s - HALF].astype(f32)
        stage[s] = (partial[s] + pltpu.roll(jnp.where(keep, theirs, mine), 64, 1)).astype(bf16)
    copies[1].start()
    for copy in later + copies:
        copy.wait()


def shards(stiffness, prolong, columns, counts, aggregate, coarse_slots, requests):
    rows, slot_count, dofs, width = stiffness.shape
    coarse = prolong.shape[2] // dofs
    n_dom = lax.axis_size("dom")
    n_field = lax.axis_size("field")
    q = requests.shape[2]
    n_ext = rows + n_dom * q
    limit = pltpu.CompilerParams(vmem_limit_bytes=24 * 2**20)
    own_flat = prolong[:, 0, :]
    other_flat = lax.ppermute(own_flat, "field", [(0, 1), (1, 0)])
    n_words = -(-(rows + 2 + n_dom) // 8) * 8
    integers = lambda *shape: VMEM(shape, jnp.int32)
    picked, own_copy, words, last_row = pl.pallas_call(
        functools.partial(prepare_kernel, n_dom, q),
        out_shape=(VMEM(((n_dom - 1) * q, own_flat.shape[1]), bf16), VMEM(own_flat.shape, bf16),
                   integers(n_words, 128), VMEM((slot_count, dofs, width), bf16)),
        in_specs=[spec(pl.ANY)] * 7,
        out_specs=(spec(VMEM),) * 4,
        scratch_shapes=[integers(rows, slot_count), integers(rows, slot_count), integers(1, rows), integers(1, rows),
                        integers(1, n_dom, q), pltpu.SemaphoreType.DMA((7,))],
        compiler_params=limit,
    )(*map(in_hbm, (own_flat, columns, coarse_slots, counts, aggregate[None], requests, stiffness)))
    g_own, g_other = [], []
    for s in range(1, n_dom):
        part = picked[(s - 1) * q : s * q]
        g_own.append(lax.ppermute(part, "dom", shift_pairs(n_dom, s)))
        pairs = [(d * n_field + f, ((d + s) % n_dom) * n_field + 1 - f) for d in range(n_dom) for f in range(n_field)]
        g_other.append(lax.ppermute(part, ("dom", "field"), pairs))
    g_own = jnp.concatenate(g_own, axis=0)
    g_other = jnp.concatenate(g_other, axis=0)
    as_blocks = lambda x: in_vmem(x.reshape(x.shape[0], dofs, coarse))
    own, other = as_blocks(own_copy), as_blocks(other_flat)
    g_own, g_other = in_vmem(g_own), in_vmem(g_other)
    block = lambda *lead: (*lead, coarse, 2 * coarse)
    words, restricted, restricted_early = pl.pallas_call(
        early_kernel,
        out_shape=(SMEM(words.shape, jnp.int32), VMEM((slot_count, coarse, width), bf16),
                   VMEM((EARLY * slot_count, coarse, width), bf16)),
        in_specs=[spec(VMEM)] * 3 + [spec(pl.ANY)],
        out_specs=(spec(SMEM), spec(VMEM), spec(VMEM)),
        scratch_shapes=[VMEM((EARLY, slot_count, dofs, width), bf16), pltpu.SemaphoreType.DMA(()),
                        pltpu.SemaphoreType.DMA((EARLY,))],
        compiler_params=limit,
        cost_estimate=pl.CostEstimate(flops=10**7, bytes_accessed=10**6, transcendentals=0),
    )(in_vmem(words), in_vmem(last_row), own, in_hbm(stiffness))
    words = pltpu.with_memory_space_constraint(words, SMEM)
    restricted, restricted_early = in_vmem(restricted), in_vmem(restricted_early)
    acc = VMEM(block(2 * HALF), f32)
    table, own_part = pl.pallas_call(
        functools.partial(own_spill_kernel, n_dom, q),
        out_shape=(VMEM((n_ext, width, 2 * coarse), bf16), VMEM(block(HALF), bf16)),
        in_specs=[spec(SMEM)] + [spec(VMEM)] * 3,
        out_specs=(spec(VMEM), spec(VMEM)),
        scratch_shapes=[acc, VMEM((g_own.shape[0] * dofs // 2, 128), f32), VMEM((dofs, 128), f32)],
        compiler_params=limit,
        cost_estimate=pl.CostEstimate(flops=10**7, bytes_accessed=10**6, transcendentals=0),
    )(words, restricted, own, g_own)
    to_next = shift_pairs(lax.axis_size("blk"), 1)
    own_part = lax.ppermute(own_part, "blk", to_next)
    table, other_part = pl.pallas_call(
        functools.partial(other_spill_kernel, n_dom, q),
        out_shape=(VMEM((n_ext, width, 2 * coarse), bf16), VMEM(block(HALF), bf16)),
        in_specs=[spec(SMEM)] + [spec(VMEM)] * 4,
        out_specs=(spec(VMEM), spec(VMEM)),
        scratch_shapes=[acc, VMEM((g_own.shape[0] * dofs // 2, 128), f32), VMEM((dofs, 128), f32)],
        input_output_aliases={4: 0},
        compiler_params=limit,
        cost_estimate=pl.CostEstimate(flops=10**7, bytes_accessed=10**6, transcendentals=0),
    )(words, restricted, other, g_other, in_vmem(table))
    other_part = lax.ppermute(other_part, "blk", to_next)
    out_shape = jax.ShapeDtypeStruct(block(NC_DEV, CSLOT), bf16)
    lead = -(-EARLY * slot_count // UNROLL) * UNROLL
    later_rows, partial = pl.pallas_call(
        functools.partial(main_kernel, lead),
        out_shape=(VMEM(block(NC_DEV - 1, CSLOT), bf16), VMEM(block(CSLOT), f32)),
        in_specs=[spec(SMEM), spec(pl.ANY)] + [spec(VMEM)] * 3,
        out_specs=(spec(VMEM),) * 2,
        scratch_shapes=[SMEM((lead + rows * AVGNZ + UNROLL + slot_count,), jnp.int32),
                        VMEM(((rows - 1 - EARLY) * slot_count, dofs, width), bf16), VMEM((rows, coarse, dofs), bf16),
                        VMEM(block(NC_DEV * CSLOT + 1), f32), pltpu.SemaphoreType.DMA((rows,))],
        compiler_params=limit,
        cost_estimate=pl.CostEstimate(flops=10**9, bytes_accessed=10**7, transcendentals=0),
    )(words, in_hbm(stiffness), own, restricted_early, in_vmem(table))
    return pl.pallas_call(
        final_kernel,
        out_shape=out_shape,
        in_specs=[spec(VMEM)] * 4,
        out_specs=spec(pl.ANY),
        scratch_shapes=[VMEM(block(CSLOT), bf16), pltpu.SemaphoreType.DMA((NC_DEV + 1,))],
        compiler_params=limit,
    )(in_vmem(partial), in_vmem(own_part), in_vmem(other_part), in_vmem(later_rows))


def solution(mesh):
    in_specs = (
        P(("dom", "blk"), None, "field", None),
        P(("dom", "blk"), "field", None),
        P(("dom", "blk"), None),
        P(("dom", "blk"), None),
        P(("dom", "blk")),
        P(("dom", "blk"), None),
        P(("dom", "blk"), None, None),
    )
    out_specs = P(("dom", "blk"), None, "field", None)
    return jax.shard_map(shards, mesh=mesh, in_specs=in_specs, out_specs=out_specs, check_vma=False)
```

```python
import functools

import jax
import jax.numpy as jnp
from jax import lax
from jax.experimental import pallas as pl
from jax.experimental.pallas import tpu as pltpu
from jax.sharding import PartitionSpec as P

CSLOT = 27
NC_DEV = 4
HALF = 14
AVGNZ = 16
CHUNK = 64
REST = 16
FIRST = 32
EARLY = 2
COLUMN_BIT = 10
SEG_BIT = 16
UNUSED = NC_DEV * CSLOT

VMEM = pltpu.VMEM
SMEM = pltpu.SMEM
f32 = jnp.float32
bf16 = jnp.bfloat16


def in_vmem(x):
    return pltpu.with_memory_space_constraint(x, VMEM)


def in_hbm(x):
    return pltpu.with_memory_space_constraint(x, pltpu.HBM)


def spec(space):
    return pl.BlockSpec(memory_space=space)


def shift_pairs(n, by):
    return [(i, (i + by) % n) for i in range(n)]


def prepare_kernel(n_dom, q, flat, columns, slots, counts, aggregate, requests, stiffness, picked, copied, words,
                   last_row, columns_v, slots_v, counts_v, aggregate_v, requests_v, sems):
    rows, slot_count = columns.shape
    pairs = ((flat, copied), (requests, requests_v), (columns, columns_v), (slots, slots_v), (counts, counts_v),
             (aggregate, aggregate_v), (stiffness.at[rows - 1], last_row))
    copies = [pltpu.make_async_copy(source, target, sems.at[i]) for i, (source, target) in enumerate(pairs)]
    for copy in copies:
        copy.start()
    me = lax.axis_index("dom")
    lane = lax.broadcasted_iota(jnp.int32, (1, rows), 1)
    block = lax.broadcasted_iota(jnp.int32, (rows, slot_count), 0) * slot_count
    block = block + lax.broadcasted_iota(jnp.int32, (rows, slot_count), 1)
    copies[0].wait()
    copies[1].wait()
    hot = []
    for s in range(1, n_dom):
        to = lax.rem(me + s, n_dom)
        asked = requests_v[0, pl.ds(to, 1), :]
        for r in range(q):
            hot.append((lane == asked[:, r : r + 1]).astype(f32))
    hot = jnp.concatenate(hot, axis=0).astype(bf16)
    picked[...] = jnp.dot(hot, copied[...], preferred_element_type=f32).astype(bf16)
    for copy in copies[2:6]:
        copy.wait()
    words[0:rows, 0:slot_count] = block + (columns_v[...] << COLUMN_BIT) + (slots_v[...] << SEG_BIT)
    words[rows : rows + 1, 0:rows] = counts_v[...]
    words[rows + 1 : rows + 2, 0:rows] = aggregate_v[...]
    words[rows + 2 : rows + 2 + n_dom, 0:q] = requests_v[0]
    copies[6].wait()


def block_of(word):
    return word & (2**COLUMN_BIT - 1)


def column_of(word):
    return (word >> COLUMN_BIT) & (2 ** (SEG_BIT - COLUMN_BIT) - 1)


def early_kernel(words_v, last_row, own, stiffness, words, restricted, restricted_early, row_buf, sem, sems):
    slot_count = last_row.shape[0]
    copy = pltpu.make_async_copy(words_v, words, sem)
    copy.start()
    rows = [pltpu.make_async_copy(stiffness.at[i], row_buf.at[i], sems.at[i]) for i in range(EARLY)]
    for row in rows:
        row.start()
    restrict = own[own.shape[0] - 1].T
    for k in range(slot_count):
        restricted[k] = jnp.dot(restrict, last_row[k], preferred_element_type=f32).astype(bf16)
    copy.wait()
    for i in range(EARLY):
        restrict = own[i].T
        rows[i].wait()
        for k in range(slot_count):
            y = jnp.dot(restrict, row_buf[i, k], preferred_element_type=f32)
            restricted_early[i * slot_count + k] = y.astype(bf16)


def unfold(flat, tiles, lines, dofs):
    count, size = flat.shape
    wide = flat[...].astype(f32)
    for t in range(size // 128):
        tiles[t * count : (t + 1) * count] = wide[:, t * 128 : (t + 1) * 128]
    blocks = []
    for r in range(count):
        pairs = tiles[pl.ds(r, dofs // 2, stride=count)]
        lines[pl.ds(0, dofs // 2, stride=2)] = pairs
        lines[pl.ds(1, dofs // 2, stride=2)] = pltpu.roll(pairs, 64, 1)
        blocks.append(lines[:, 0:64].astype(bf16))
    return blocks


def lane_half():
    return lax.broadcasted_iota(jnp.int32, (64, 128), 1) < 64


def corner(field, dofs, value):
    zero = jnp.zeros_like(value)
    left = jnp.concatenate([value, zero], axis=1)
    right = jnp.concatenate([zero, value], axis=1)
    return pl.multiple_of(field * dofs, dofs), jnp.where(field == 0, left, right)


def fill_table(n_dom, q, field, words, blocks, ghosts, table, tiles, lines):
    rows, dofs = blocks.shape[:2]
    me = lax.axis_index("dom")

    def put(j, value):
        start, lines = corner(field, dofs, value)
        table[j, pl.ds(start, dofs)] = lines

    for j in range(rows):
        put(j, blocks[j])
    ghosts = unfold(ghosts, tiles, lines, dofs)
    for s in range(1, n_dom):
        source = lax.rem(me + n_dom - s, n_dom)
        for r in range(q):
            put(rows + source * q + r, ghosts[(s - 1) * q + r])
    for r in range(q):
        put(rows + me * q + r, blocks[words[rows + 2 + me, r]])


def spill_half(rows, field, words, restricted, table, out, acc):
    slot_count = restricted.shape[0]
    last = rows - 1
    acc[...] = jnp.zeros_like(acc)
    live = words[rows, last]
    listed = [words[last, k] for k in range(slot_count)]
    products = [
        jnp.dot(restricted[k], table[column_of(listed[k])], preferred_element_type=f32) for k in range(slot_count)
    ]
    for k in range(slot_count):
        acc[jnp.where(k < live, listed[k] >> SEG_BIT, CSLOT)] += products[k]
    keep = lane_half() == (field == 0)
    for s in range(HALF):
        block = acc[s]
        if s + HALF < CSLOT:
            block = jnp.where(keep, block, pltpu.roll(acc[s + HALF], 64, 1))
        out[s] = block.astype(bf16)


def own_spill_kernel(n_dom, q, words, restricted, own, ghosts, table, out, acc, tiles, lines):
    field = lax.axis_index("field")
    table[...] = jnp.zeros_like(table)
    fill_table(n_dom, q, field, words, own, ghosts, table, tiles, lines)
    spill_half(own.shape[0], field, words, restricted, table, out, acc)


def other_spill_kernel(n_dom, q, words, restricted, other, ghosts, _, table, out, acc, tiles, lines):
    field = 1 - lax.axis_index("field")
    fill_table(n_dom, q, field, words, other, ghosts, table, tiles, lines)
    spill_half(other.shape[0], field, words, restricted, table, out, acc)


def fill_list(words, listed, rows, slot_count, lead):
    base = 0
    for i in range(rows - 1):
        if i == EARLY:
            for k in range(FIRST):
                listed[base + k] = UNUSED << SEG_BIT
            first_length = base
            base = lead
        offset = (words[rows + 1, i] * CSLOT) << SEG_BIT
        for k in range(slot_count):
            listed[base + k] = words[i, k] + offset
        base = base + words[rows, i]
    for k in range(REST):
        listed[base + k] = (UNUSED << SEG_BIT) + (rows - 2) * slot_count
    return first_length, base - lead


def main_kernel(lead, words, stiffness, own, restricted_early, table, later_rows, first_row, listed, stiff, restrict, acc,
                sems):
    rows, slot_count = stiffness.shape[:2]

    def row_copy(i):
        part = pl.ds((i - EARLY) * slot_count, slot_count)
        return pltpu.make_async_copy(stiffness.at[i], stiff.at[part], sems.at[i])

    for i in range(EARLY, rows - 1):
        row_copy(i).start()
    first_length, second_length = fill_list(words, listed, rows, slot_count, lead)
    for i in range(EARLY, rows - 1):
        restrict[i] = own[i].T
    acc[...] = jnp.zeros_like(acc)

    def add(taken, restricted):
        products = [jnp.dot(y, table[column_of(w)], preferred_element_type=f32) for w, y in zip(taken, restricted)]
        for w, z in zip(taken, products):
            acc[w >> SEG_BIT] += z

    @pl.loop(0, (first_length + FIRST - 1) // FIRST)
    def _(c):
        taken = [listed[c * FIRST + u] for u in range(FIRST)]
        add(taken, [restricted_early[block_of(w)] for w in taken])

    def chunk(start, size, arrived):
        taken = [listed[lead + start + u] for u in range(size)]
        blocks = [block_of(w) for w in taken]
        needed = blocks[size - 1] // slot_count + 1

        @pl.loop(arrived, needed)
        def _(i):
            row_copy(i).wait()

        add(taken, [
            jnp.dot(restrict[b // slot_count], stiff[b - EARLY * slot_count], preferred_element_type=f32).astype(bf16)
            for b in blocks
        ])
        return needed

    whole = second_length // CHUNK
    left = second_length - whole * CHUNK
    arrived = lax.fori_loop(0, whole, lambda c, got: chunk(c * CHUNK, CHUNK, got), EARLY)
    lax.fori_loop(0, (left + REST - 1) // REST, lambda c, got: chunk(whole * CHUNK + c * REST, REST, got), arrived)
    for c in range(1, NC_DEV):
        later_rows[c - 1] = acc[c * CSLOT : (c + 1) * CSLOT].astype(bf16)
    first_row[...] = acc[0:CSLOT]


def final_kernel(partial, own_part, other_part, later_rows, out, stage, sems):
    keep = lane_half() == (lax.axis_index("field") == 0)
    later = [pltpu.make_async_copy(later_rows.at[c - 1], out.at[c], sems.at[c]) for c in range(1, NC_DEV)]
    for copy in later:
        copy.start()
    copies = [pltpu.make_async_copy(stage.at[pl.ds(s, n)], out.at[0, pl.ds(s, n)], sem)
              for s, n, sem in ((0, HALF, sems.at[0]), (HALF, CSLOT - HALF, sems.at[NC_DEV]))]
    for s in range(HALF):
        mine, theirs = own_part[s].astype(f32), other_part[s].astype(f32)
        stage[s] = (partial[s] + jnp.where(keep, mine, theirs)).astype(bf16)
    copies[0].start()
    for s in range(HALF, CSLOT):
        mine, theirs = own_part[s - HALF].astype(f32), other_part[s - HALF].astype(f32)
        stage[s] = (partial[s] + pltpu.roll(jnp.where(keep, theirs, mine), 64, 1)).astype(bf16)
    copies[1].start()
    for copy in later + copies:
        copy.wait()


def shards(stiffness, prolong, columns, counts, aggregate, coarse_slots, requests):
    rows, slot_count, dofs, width = stiffness.shape
    coarse = prolong.shape[2] // dofs
    n_dom = lax.axis_size("dom")
    n_field = lax.axis_size("field")
    q = requests.shape[2]
    n_ext = rows + n_dom * q
    limit = pltpu.CompilerParams(vmem_limit_bytes=24 * 2**20)
    own_flat = prolong[:, 0, :]
    other_flat = lax.ppermute(own_flat, "field", [(0, 1), (1, 0)])
    n_words = -(-(rows + 2 + n_dom) // 8) * 8
    integers = lambda *shape: VMEM(shape, jnp.int32)
    picked, own_copy, words, last_row = pl.pallas_call(
        functools.partial(prepare_kernel, n_dom, q),
        out_shape=(VMEM(((n_dom - 1) * q, own_flat.shape[1]), bf16), VMEM(own_flat.shape, bf16),
                   integers(n_words, 128), VMEM((slot_count, dofs, width), bf16)),
        in_specs=[spec(pl.ANY)] * 7,
        out_specs=(spec(VMEM),) * 4,
        scratch_shapes=[integers(rows, slot_count), integers(rows, slot_count), integers(1, rows), integers(1, rows),
                        integers(1, n_dom, q), pltpu.SemaphoreType.DMA((7,))],
        compiler_params=limit,
    )(*map(in_hbm, (own_flat, columns, coarse_slots, counts, aggregate[None], requests, stiffness)))
    g_own, g_other = [], []
    for s in range(1, n_dom):
        part = picked[(s - 1) * q : s * q]
        g_own.append(lax.ppermute(part, "dom", shift_pairs(n_dom, s)))
        pairs = [(d * n_field + f, ((d + s) % n_dom) * n_field + 1 - f) for d in range(n_dom) for f in range(n_field)]
        g_other.append(lax.ppermute(part, ("dom", "field"), pairs))
    g_own = jnp.concatenate(g_own, axis=0)
    g_other = jnp.concatenate(g_other, axis=0)
    as_blocks = lambda x: in_vmem(x.reshape(x.shape[0], dofs, coarse))
    own, other = as_blocks(own_copy), as_blocks(other_flat)
    g_own, g_other = in_vmem(g_own), in_vmem(g_other)
    block = lambda *lead: (*lead, coarse, 2 * coarse)
    words, restricted, restricted_early = pl.pallas_call(
        early_kernel,
        out_shape=(SMEM(words.shape, jnp.int32), VMEM((slot_count, coarse, width), bf16),
                   VMEM((EARLY * slot_count, coarse, width), bf16)),
        in_specs=[spec(VMEM)] * 3 + [spec(pl.ANY)],
        out_specs=(spec(SMEM), spec(VMEM), spec(VMEM)),
        scratch_shapes=[VMEM((EARLY, slot_count, dofs, width), bf16), pltpu.SemaphoreType.DMA(()),
                        pltpu.SemaphoreType.DMA((EARLY,))],
        compiler_params=limit,
        cost_estimate=pl.CostEstimate(flops=10**7, bytes_accessed=10**6, transcendentals=0),
    )(in_vmem(words), in_vmem(last_row), own, in_hbm(stiffness))
    words = pltpu.with_memory_space_constraint(words, SMEM)
    restricted, restricted_early = in_vmem(restricted), in_vmem(restricted_early)
    acc = VMEM(block(2 * HALF), f32)
    table, own_part = pl.pallas_call(
        functools.partial(own_spill_kernel, n_dom, q),
        out_shape=(VMEM((n_ext, width, 2 * coarse), bf16), VMEM(block(HALF), bf16)),
        in_specs=[spec(SMEM)] + [spec(VMEM)] * 3,
        out_specs=(spec(VMEM), spec(VMEM)),
        scratch_shapes=[acc, VMEM((g_own.shape[0] * dofs // 2, 128), f32), VMEM((dofs, 128), f32)],
        compiler_params=limit,
        cost_estimate=pl.CostEstimate(flops=10**7, bytes_accessed=10**6, transcendentals=0),
    )(words, restricted, own, g_own)
    to_next = shift_pairs(lax.axis_size("blk"), 1)
    own_part = lax.ppermute(own_part, "blk", to_next)
    table, other_part = pl.pallas_call(
        functools.partial(other_spill_kernel, n_dom, q),
        out_shape=(VMEM((n_ext, width, 2 * coarse), bf16), VMEM(block(HALF), bf16)),
        in_specs=[spec(SMEM)] + [spec(VMEM)] * 4,
        out_specs=(spec(VMEM), spec(VMEM)),
        scratch_shapes=[acc, VMEM((g_own.shape[0] * dofs // 2, 128), f32), VMEM((dofs, 128), f32)],
        input_output_aliases={4: 0},
        compiler_params=limit,
        cost_estimate=pl.CostEstimate(flops=10**7, bytes_accessed=10**6, transcendentals=0),
    )(words, restricted, other, g_other, in_vmem(table))
    other_part = lax.ppermute(other_part, "blk", to_next)
    out_shape = jax.ShapeDtypeStruct(block(NC_DEV, CSLOT), bf16)
    lead = EARLY * slot_count + FIRST
    later_rows, partial = pl.pallas_call(
        functools.partial(main_kernel, lead),
        out_shape=(VMEM(block(NC_DEV - 1, CSLOT), bf16), VMEM(block(CSLOT), f32)),
        in_specs=[spec(SMEM), spec(pl.ANY)] + [spec(VMEM)] * 3,
        out_specs=(spec(VMEM),) * 2,
        scratch_shapes=[SMEM((lead + rows * AVGNZ + REST + slot_count,), jnp.int32),
                        VMEM(((rows - 1 - EARLY) * slot_count, dofs, width), bf16), VMEM((rows, coarse, dofs), bf16),
                        VMEM(block(NC_DEV * CSLOT + 1), f32), pltpu.SemaphoreType.DMA((rows,))],
        compiler_params=limit,
        cost_estimate=pl.CostEstimate(flops=10**9, bytes_accessed=10**7, transcendentals=0),
    )(words, in_hbm(stiffness), own, restricted_early, in_vmem(table))
    return pl.pallas_call(
        final_kernel,
        out_shape=out_shape,
        in_specs=[spec(VMEM)] * 4,
        out_specs=spec(pl.ANY),
        scratch_shapes=[VMEM(block(CSLOT), bf16), pltpu.SemaphoreType.DMA((NC_DEV + 1,))],
        compiler_params=limit,
    )(in_vmem(partial), in_vmem(own_part), in_vmem(other_part), in_vmem(later_rows))


def solution(mesh):
    in_specs = (
        P(("dom", "blk"), None, "field", None),
        P(("dom", "blk"), "field", None),
        P(("dom", "blk"), None),
        P(("dom", "blk"), None),
        P(("dom", "blk")),
        P(("dom", "blk"), None),
        P(("dom", "blk"), None, None),
    )
    out_specs = P(("dom", "blk"), None, "field", None)
    return jax.shard_map(shards, mesh=mesh, in_specs=in_specs, out_specs=out_specs, check_vma=False)
```

```python
import functools

import jax
import jax.numpy as jnp
from jax import lax
from jax.experimental import pallas as pl
from jax.experimental.pallas import tpu as pltpu
from jax.sharding import PartitionSpec as P

CSLOT = 27
NC_DEV = 4
HALF = 14
AVGNZ = 16
CHUNK = 96
GROUP = 16
REST = 16
FIRST = 32
EARLY = 2
COLUMN_BIT = 10
SEG_BIT = 16
UNUSED = NC_DEV * CSLOT

VMEM = pltpu.VMEM
SMEM = pltpu.SMEM
f32 = jnp.float32
bf16 = jnp.bfloat16


def in_vmem(x):
    return pltpu.with_memory_space_constraint(x, VMEM)


def in_hbm(x):
    return pltpu.with_memory_space_constraint(x, pltpu.HBM)


def spec(space):
    return pl.BlockSpec(memory_space=space)


def shift_pairs(n, by):
    return [(i, (i + by) % n) for i in range(n)]


def prepare_kernel(n_dom, q, flat, columns, slots, counts, aggregate, requests, stiffness, picked, copied, words,
                   last_row, columns_v, slots_v, counts_v, aggregate_v, requests_v, sems):
    rows, slot_count = columns.shape
    pairs = ((flat, copied), (requests, requests_v), (columns, columns_v), (slots, slots_v), (counts, counts_v),
             (aggregate, aggregate_v), (stiffness.at[rows - 1], last_row))
    copies = [pltpu.make_async_copy(source, target, sems.at[i]) for i, (source, target) in enumerate(pairs)]
    for copy in copies:
        copy.start()
    me = lax.axis_index("dom")
    lane = lax.broadcasted_iota(jnp.int32, (1, rows), 1)
    block = lax.broadcasted_iota(jnp.int32, (rows, slot_count), 0) * slot_count
    block = block + lax.broadcasted_iota(jnp.int32, (rows, slot_count), 1)
    copies[0].wait()
    copies[1].wait()
    hot = []
    for s in range(1, n_dom):
        to = lax.rem(me + s, n_dom)
        asked = requests_v[0, pl.ds(to, 1), :]
        for r in range(q):
            hot.append((lane == asked[:, r : r + 1]).astype(f32))
    hot = jnp.concatenate(hot, axis=0).astype(bf16)
    picked[...] = jnp.dot(hot, copied[...], preferred_element_type=f32).astype(bf16)
    for copy in copies[2:6]:
        copy.wait()
    words[0:rows, 0:slot_count] = block + (columns_v[...] << COLUMN_BIT) + (slots_v[...] << SEG_BIT)
    words[rows : rows + 1, 0:rows] = counts_v[...]
    words[rows + 1 : rows + 2, 0:rows] = aggregate_v[...]
    words[rows + 2 : rows + 2 + n_dom, 0:q] = requests_v[0]
    copies[6].wait()


def block_of(word):
    return word & (2**COLUMN_BIT - 1)


def column_of(word):
    return (word >> COLUMN_BIT) & (2 ** (SEG_BIT - COLUMN_BIT) - 1)


def early_kernel(words_v, last_row, own, stiffness, words, restricted, restricted_early, row_buf, sem, sems):
    slot_count = last_row.shape[0]
    copy = pltpu.make_async_copy(words_v, words, sem)
    copy.start()
    rows = [pltpu.make_async_copy(stiffness.at[i], row_buf.at[i], sems.at[i]) for i in range(EARLY)]
    for row in rows:
        row.start()
    restrict = own[own.shape[0] - 1].T
    for k in range(slot_count):
        restricted[k] = jnp.dot(restrict, last_row[k], preferred_element_type=f32).astype(bf16)
    copy.wait()
    for i in range(EARLY):
        restrict = own[i].T
        rows[i].wait()
        for k in range(slot_count):
            y = jnp.dot(restrict, row_buf[i, k], preferred_element_type=f32)
            restricted_early[i * slot_count + k] = y.astype(bf16)


def unfold(flat, tiles, lines, dofs):
    count, size = flat.shape
    wide = flat[...].astype(f32)
    for t in range(size // 128):
        tiles[t * count : (t + 1) * count] = wide[:, t * 128 : (t + 1) * 128]
    blocks = []
    for r in range(count):
        pairs = tiles[pl.ds(r, dofs // 2, stride=count)]
        lines[pl.ds(0, dofs // 2, stride=2)] = pairs
        lines[pl.ds(1, dofs // 2, stride=2)] = pltpu.roll(pairs, 64, 1)
        blocks.append(lines[0:dofs, 0:64].astype(bf16))
    return blocks


def lane_half():
    return lax.broadcasted_iota(jnp.int32, (64, 128), 1) < 64


def corner(field, dofs, value):
    zero = jnp.zeros_like(value)
    left = jnp.concatenate([value, zero], axis=1)
    right = jnp.concatenate([zero, value], axis=1)
    return pl.multiple_of(field * dofs, dofs), jnp.where(field == 0, left, right)


def fill_table(n_dom, q, field, words, blocks, ghosts, table, tiles, lines):
    rows, dofs = blocks.shape[:2]
    me = lax.axis_index("dom")

    def put(j, value):
        start, lines = corner(field, dofs, value)
        table[j, pl.ds(start, dofs)] = lines

    for j in range(rows):
        put(j, blocks[j])
    ghosts = unfold(ghosts, tiles, lines, dofs)
    for s in range(1, n_dom):
        source = lax.rem(me + n_dom - s, n_dom)
        for r in range(q):
            put(rows + source * q + r, ghosts[(s - 1) * q + r])
    for r in range(q):
        put(rows + me * q + r, blocks[words[rows + 2 + me, r]])


def spill_half(rows, field, words, restricted, table, out, acc):
    slot_count = restricted.shape[0]
    last = rows - 1
    acc[...] = jnp.zeros_like(acc)
    live = words[rows, last]
    listed = [words[last, k] for k in range(slot_count)]
    products = [
        jnp.dot(restricted[k], table[column_of(listed[k])], preferred_element_type=f32) for k in range(slot_count)
    ]
    for k in range(slot_count):
        acc[jnp.where(k < live, listed[k] >> SEG_BIT, CSLOT)] += products[k]
    keep = lane_half() == (field == 0)
    for s in range(HALF):
        block = acc[s]
        if s + HALF < CSLOT:
            block = jnp.where(keep, block, pltpu.roll(acc[s + HALF], 64, 1))
        out[s] = block.astype(bf16)


def own_spill_kernel(n_dom, q, words, restricted, own, ghosts, table, out, acc, tiles, lines):
    field = lax.axis_index("field")
    table[...] = jnp.zeros_like(table)
    fill_table(n_dom, q, field, words, own, ghosts, table, tiles, lines)
    spill_half(own.shape[0], field, words, restricted, table, out, acc)


def other_spill_kernel(n_dom, q, words, restricted, other, ghosts, _, table, out, acc, tiles, lines):
    field = 1 - lax.axis_index("field")
    fill_table(n_dom, q, field, words, other, ghosts, table, tiles, lines)
    spill_half(other.shape[0], field, words, restricted, table, out, acc)


def fill_list(words, listed, rows, slot_count, lead):
    base = 0
    for i in range(rows - 1):
        if i == EARLY:
            for k in range(FIRST):
                listed[base + k] = UNUSED << SEG_BIT
            first_length = base
            base = lead
        offset = (words[rows + 1, i] * CSLOT) << SEG_BIT
        for k in range(slot_count):
            listed[base + k] = words[i, k] + offset
        base = base + words[rows, i]
    for k in range(REST):
        listed[base + k] = (UNUSED << SEG_BIT) + (rows - 2) * slot_count
    return first_length, base - lead


def main_kernel(lead, words, stiffness, own, restricted_early, table, later_rows, first_row, listed, stiff, restrict, acc,
                sems):
    rows, slot_count = stiffness.shape[:2]

    def row_copy(i):
        part = pl.ds((i - EARLY) * slot_count, slot_count)
        return pltpu.make_async_copy(stiffness.at[i], stiff.at[part], sems.at[i])

    for i in range(EARLY, rows - 1):
        row_copy(i).start()
    first_length, second_length = fill_list(words, listed, rows, slot_count, lead)
    for i in range(EARLY, rows - 1):
        restrict[i] = own[i].T
    acc[...] = jnp.zeros_like(acc)

    def add(taken, restricted):
        products = [jnp.dot(y, table[column_of(w)], preferred_element_type=f32) for w, y in zip(taken, restricted)]
        for w, z in zip(taken, products):
            acc[w >> SEG_BIT] += z

    @pl.loop(0, (first_length + FIRST - 1) // FIRST)
    def _(c):
        taken = [listed[c * FIRST + u] for u in range(FIRST)]
        add(taken, [restricted_early[block_of(w)] for w in taken])

    def chunk(start, size, arrived):
        taken = [listed[lead + start + u] for u in range(size)]
        blocks = [block_of(w) for w in taken]
        needed = blocks[size - 1] // slot_count + 1

        @pl.loop(arrived, needed)
        def _(i):
            row_copy(i).wait()

        held = None
        for g in range(0, size, GROUP):
            restricted = [
                jnp.dot(restrict[b // slot_count], stiff[b - EARLY * slot_count], preferred_element_type=f32).astype(bf16)
                for b in blocks[g : g + GROUP]
            ]
            if held is not None:
                add(*held)
            held = taken[g : g + GROUP], restricted
        add(*held)
        return needed

    whole = second_length // CHUNK
    small = (second_length - whole * CHUNK + REST - 1) // REST
    arrived = lax.fori_loop(0, small, lambda c, got: chunk(c * REST, REST, got), EARLY)
    lax.fori_loop(0, whole, lambda c, got: chunk(small * REST + c * CHUNK, CHUNK, got), arrived)
    for c in range(1, NC_DEV):
        later_rows[c - 1] = acc[c * CSLOT : (c + 1) * CSLOT].astype(bf16)
    first_row[...] = acc[0:CSLOT]


def final_kernel(partial, own_part, other_part, later_rows, out, stage, sems):
    keep = lane_half() == (lax.axis_index("field") == 0)
    later = [pltpu.make_async_copy(later_rows.at[c - 1], out.at[c], sems.at[c]) for c in range(1, NC_DEV)]
    for copy in later:
        copy.start()
    copies = [pltpu.make_async_copy(stage.at[pl.ds(s, n)], out.at[0, pl.ds(s, n)], sem)
              for s, n, sem in ((0, HALF, sems.at[0]), (HALF, CSLOT - HALF, sems.at[NC_DEV]))]
    for s in range(HALF):
        mine, theirs = own_part[s].astype(f32), other_part[s].astype(f32)
        stage[s] = (partial[s] + jnp.where(keep, mine, theirs)).astype(bf16)
    copies[0].start()
    for s in range(HALF, CSLOT):
        mine, theirs = own_part[s - HALF].astype(f32), other_part[s - HALF].astype(f32)
        stage[s] = (partial[s] + pltpu.roll(jnp.where(keep, theirs, mine), 64, 1)).astype(bf16)
    copies[1].start()
    for copy in later + copies:
        copy.wait()


def shards(stiffness, prolong, columns, counts, aggregate, coarse_slots, requests):
    rows, slot_count, dofs, width = stiffness.shape
    coarse = prolong.shape[2] // dofs
    n_dom = lax.axis_size("dom")
    n_field = lax.axis_size("field")
    q = requests.shape[2]
    n_ext = rows + n_dom * q
    limit = pltpu.CompilerParams(vmem_limit_bytes=24 * 2**20)
    own_flat = prolong[:, 0, :]
    other_flat = lax.ppermute(own_flat, "field", [(0, 1), (1, 0)])
    n_words = -(-(rows + 2 + n_dom) // 8) * 8
    integers = lambda *shape: VMEM(shape, jnp.int32)
    picked, own_copy, words, last_row = pl.pallas_call(
        functools.partial(prepare_kernel, n_dom, q),
        out_shape=(VMEM(((n_dom - 1) * q, own_flat.shape[1]), bf16), VMEM(own_flat.shape, bf16),
                   integers(n_words, 128), VMEM((slot_count, dofs, width), bf16)),
        in_specs=[spec(pl.ANY)] * 7,
        out_specs=(spec(VMEM),) * 4,
        scratch_shapes=[integers(rows, slot_count), integers(rows, slot_count), integers(1, rows), integers(1, rows),
                        integers(1, n_dom, q), pltpu.SemaphoreType.DMA((7,))],
        compiler_params=limit,
    )(*map(in_hbm, (own_flat, columns, coarse_slots, counts, aggregate[None], requests, stiffness)))
    g_own, g_other = [], []
    for s in range(1, n_dom):
        part = picked[(s - 1) * q : s * q]
        g_own.append(lax.ppermute(part, "dom", shift_pairs(n_dom, s)))
        pairs = [(d * n_field + f, ((d + s) % n_dom) * n_field + 1 - f) for d in range(n_dom) for f in range(n_field)]
        g_other.append(lax.ppermute(part, ("dom", "field"), pairs))
    g_own = jnp.concatenate(g_own, axis=0)
    g_other = jnp.concatenate(g_other, axis=0)
    as_blocks = lambda x: in_vmem(x.reshape(x.shape[0], dofs, coarse))
    own, other = as_blocks(own_copy), as_blocks(other_flat)
    g_own, g_other = in_vmem(g_own), in_vmem(g_other)
    block = lambda *lead: (*lead, coarse, 2 * coarse)
    words, restricted, restricted_early = pl.pallas_call(
        early_kernel,
        out_shape=(SMEM(words.shape, jnp.int32), VMEM((slot_count, coarse, width), bf16),
                   VMEM((EARLY * slot_count, coarse, width), bf16)),
        in_specs=[spec(VMEM)] * 3 + [spec(pl.ANY)],
        out_specs=(spec(SMEM), spec(VMEM), spec(VMEM)),
        scratch_shapes=[VMEM((EARLY, slot_count, dofs, width), bf16), pltpu.SemaphoreType.DMA(()),
                        pltpu.SemaphoreType.DMA((EARLY,))],
        compiler_params=limit,
        cost_estimate=pl.CostEstimate(flops=10**7, bytes_accessed=10**6, transcendentals=0),
    )(in_vmem(words), in_vmem(last_row), own, in_hbm(stiffness))
    words = pltpu.with_memory_space_constraint(words, SMEM)
    restricted, restricted_early = in_vmem(restricted), in_vmem(restricted_early)
    acc = VMEM(block(2 * HALF), f32)
    unfolding = VMEM((g_own.shape[0] * (dofs // 2 + 4), 128), f32), VMEM((dofs + 8, 128), f32)
    table, own_part = pl.pallas_call(
        functools.partial(own_spill_kernel, n_dom, q),
        out_shape=(VMEM((n_ext, width, 2 * coarse), bf16), VMEM(block(HALF), bf16)),
        in_specs=[spec(SMEM)] + [spec(VMEM)] * 3,
        out_specs=(spec(VMEM), spec(VMEM)),
        scratch_shapes=[acc, *unfolding],
        compiler_params=limit,
        cost_estimate=pl.CostEstimate(flops=10**7, bytes_accessed=10**6, transcendentals=0),
    )(words, restricted, own, g_own)
    to_next = shift_pairs(lax.axis_size("blk"), 1)
    own_part = lax.ppermute(own_part, "blk", to_next)
    table, other_part = pl.pallas_call(
        functools.partial(other_spill_kernel, n_dom, q),
        out_shape=(VMEM((n_ext, width, 2 * coarse), bf16), VMEM(block(HALF), bf16)),
        in_specs=[spec(SMEM)] + [spec(VMEM)] * 4,
        out_specs=(spec(VMEM), spec(VMEM)),
        scratch_shapes=[acc, *unfolding],
        input_output_aliases={4: 0},
        compiler_params=limit,
        cost_estimate=pl.CostEstimate(flops=10**7, bytes_accessed=10**6, transcendentals=0),
    )(words, restricted, other, g_other, in_vmem(table))
    other_part = lax.ppermute(other_part, "blk", to_next)
    out_shape = jax.ShapeDtypeStruct(block(NC_DEV, CSLOT), bf16)
    lead = EARLY * slot_count + FIRST
    later_rows, partial = pl.pallas_call(
        functools.partial(main_kernel, lead),
        out_shape=(VMEM(block(NC_DEV - 1, CSLOT), bf16), VMEM(block(CSLOT), f32)),
        in_specs=[spec(SMEM), spec(pl.ANY)] + [spec(VMEM)] * 3,
        out_specs=(spec(VMEM),) * 2,
        scratch_shapes=[SMEM((lead + rows * AVGNZ + REST + slot_count,), jnp.int32),
                        VMEM(((rows - 1 - EARLY) * slot_count, dofs, width), bf16), VMEM((rows, coarse, dofs), bf16),
                        VMEM(block(NC_DEV * CSLOT + 1), f32), pltpu.SemaphoreType.DMA((rows,))],
        compiler_params=limit,
        cost_estimate=pl.CostEstimate(flops=10**9, bytes_accessed=10**7, transcendentals=0),
    )(words, in_hbm(stiffness), own, restricted_early, in_vmem(table))
    return pl.pallas_call(
        final_kernel,
        out_shape=out_shape,
        in_specs=[spec(VMEM)] * 4,
        out_specs=spec(pl.ANY),
        scratch_shapes=[VMEM(block(CSLOT), bf16), pltpu.SemaphoreType.DMA((NC_DEV + 1,))],
        compiler_params=limit,
    )(in_vmem(partial), in_vmem(own_part), in_vmem(other_part), in_vmem(later_rows))


def solution(mesh):
    in_specs = (
        P(("dom", "blk"), None, "field", None),
        P(("dom", "blk"), "field", None),
        P(("dom", "blk"), None),
        P(("dom", "blk"), None),
        P(("dom", "blk")),
        P(("dom", "blk"), None),
        P(("dom", "blk"), None, None),
    )
    out_specs = P(("dom", "blk"), None, "field", None)
    return jax.shard_map(shards, mesh=mesh, in_specs=in_specs, out_specs=out_specs, check_vma=False)
```

```python
import functools

import jax
import jax.numpy as jnp
from jax import lax
from jax.experimental import pallas as pl
from jax.experimental.pallas import tpu as pltpu
from jax.sharding import PartitionSpec as P

CSLOT = 27
NC_DEV = 4
HALF = 14
AVGNZ = 16
CHUNK = 96
GROUP = 16
REST = 16
FIRST = 32
EARLY = 1
COLUMN_BIT = 10
SEG_BIT = 16
UNUSED = NC_DEV * CSLOT

VMEM = pltpu.VMEM
SMEM = pltpu.SMEM
f32 = jnp.float32
bf16 = jnp.bfloat16


def in_vmem(x):
    return pltpu.with_memory_space_constraint(x, VMEM)


def in_hbm(x):
    return pltpu.with_memory_space_constraint(x, pltpu.HBM)


def spec(space):
    return pl.BlockSpec(memory_space=space)


def shift_pairs(n, by):
    return [(i, (i + by) % n) for i in range(n)]


def prepare_kernel(n_dom, q, flat, columns, slots, counts, aggregate, requests, picked, copied, words, columns_v,
                    slots_v, counts_v, aggregate_v, requests_v, sems):
    rows, slot_count = columns.shape
    pairs = ((flat, copied), (requests, requests_v), (columns, columns_v), (slots, slots_v), (counts, counts_v),
             (aggregate, aggregate_v))
    copies = [pltpu.make_async_copy(source, target, sems.at[i]) for i, (source, target) in enumerate(pairs)]
    for copy in copies:
        copy.start()
    me = lax.axis_index("dom")
    lane = lax.broadcasted_iota(jnp.int32, (1, rows), 1)
    block = lax.broadcasted_iota(jnp.int32, (rows, slot_count), 0) * slot_count
    block = block + lax.broadcasted_iota(jnp.int32, (rows, slot_count), 1)
    copies[0].wait()
    copies[1].wait()
    hot = []
    for s in range(1, n_dom):
        to = lax.rem(me + s, n_dom)
        asked = requests_v[0, pl.ds(to, 1), :]
        for r in range(q):
            hot.append((lane == asked[:, r : r + 1]).astype(f32))
    hot = jnp.concatenate(hot, axis=0).astype(bf16)
    picked[...] = jnp.dot(hot, copied[...], preferred_element_type=f32).astype(bf16)
    for copy in copies[2:6]:
        copy.wait()
    words[0:rows, 0:slot_count] = block + (columns_v[...] << COLUMN_BIT) + (slots_v[...] << SEG_BIT)
    words[rows : rows + 1, 0:rows] = counts_v[...]
    words[rows + 1 : rows + 2, 0:rows] = aggregate_v[...]
    words[rows + 2 : rows + 2 + n_dom, 0:q] = requests_v[0]


def block_of(word):
    return word & (2**COLUMN_BIT - 1)


def column_of(word):
    return (word >> COLUMN_BIT) & (2 ** (SEG_BIT - COLUMN_BIT) - 1)


def early_kernel(words_v, own, stiffness, words, restricted, restricted_early, row_buf, sem, sems):
    slot_count = stiffness.shape[1]
    chosen = [stiffness.shape[0] - 1, *range(EARLY)]
    copies = [pltpu.make_async_copy(stiffness.at[i], row_buf.at[p], sems.at[p]) for p, i in enumerate(chosen)]
    for copy in copies:
        copy.start()
    word_copy = pltpu.make_async_copy(words_v, words, sem)
    word_copy.start()
    restrict = [own[i].T for i in chosen]
    word_copy.wait()
    for p, copy in enumerate(copies):
        copy.wait()
        for k in range(slot_count):
            y = jnp.dot(restrict[p], row_buf[p, k], preferred_element_type=f32).astype(bf16)
            if p == 0:
                restricted[k] = y
            else:
                restricted_early[(p - 1) * slot_count + k] = y


def unfold(flat, tiles, lines, dofs):
    count, size = flat.shape
    wide = flat[...].astype(f32)
    for t in range(size // 128):
        tiles[t * count : (t + 1) * count] = wide[:, t * 128 : (t + 1) * 128]
    blocks = []
    for r in range(count):
        pairs = tiles[pl.ds(r, dofs // 2, stride=count)]
        lines[pl.ds(0, dofs // 2, stride=2)] = pairs
        lines[pl.ds(1, dofs // 2, stride=2)] = pltpu.roll(pairs, 64, 1)
        blocks.append(lines[0:dofs, 0:64].astype(bf16))
    return blocks


def lane_half():
    return lax.broadcasted_iota(jnp.int32, (64, 128), 1) < 64


def corner(field, dofs, value):
    zero = jnp.zeros_like(value)
    left = jnp.concatenate([value, zero], axis=1)
    right = jnp.concatenate([zero, value], axis=1)
    return pl.multiple_of(field * dofs, dofs), jnp.where(field == 0, left, right)


def fill_table(n_dom, q, field, words, blocks, ghosts, table, tiles, lines):
    rows, dofs = blocks.shape[:2]
    me = lax.axis_index("dom")

    def put(j, value):
        start, lines = corner(field, dofs, value)
        table[j, pl.ds(start, dofs)] = lines

    for j in range(rows):
        put(j, blocks[j])
    ghosts = unfold(ghosts, tiles, lines, dofs)
    for s in range(1, n_dom):
        source = lax.rem(me + n_dom - s, n_dom)
        for r in range(q):
            put(rows + source * q + r, ghosts[(s - 1) * q + r])
    for r in range(q):
        put(rows + me * q + r, blocks[words[rows + 2 + me, r]])


def spill_half(rows, field, words, restricted, table, out, acc):
    slot_count = restricted.shape[0]
    last = rows - 1
    acc[...] = jnp.zeros_like(acc)
    live = words[rows, last]
    listed = [words[last, k] for k in range(slot_count)]
    products = [
        jnp.dot(restricted[k], table[column_of(listed[k])], preferred_element_type=f32) for k in range(slot_count)
    ]
    for k in range(slot_count):
        acc[jnp.where(k < live, listed[k] >> SEG_BIT, CSLOT)] += products[k]
    keep = lane_half() == (field == 0)
    for s in range(HALF):
        block = acc[s]
        if s + HALF < CSLOT:
            block = jnp.where(keep, block, pltpu.roll(acc[s + HALF], 64, 1))
        out[s] = block.astype(bf16)


def own_spill_kernel(n_dom, q, words, restricted, own, ghosts, table, out, acc, tiles, lines):
    field = lax.axis_index("field")
    table[...] = jnp.zeros_like(table)
    fill_table(n_dom, q, field, words, own, ghosts, table, tiles, lines)
    spill_half(own.shape[0], field, words, restricted, table, out, acc)


def other_spill_kernel(n_dom, q, words, restricted, other, ghosts, _, table, out, acc, tiles, lines):
    field = 1 - lax.axis_index("field")
    fill_table(n_dom, q, field, words, other, ghosts, table, tiles, lines)
    spill_half(other.shape[0], field, words, restricted, table, out, acc)


def fill_list(words, listed, rows, slot_count, lead):
    base = 0
    for i in range(rows - 1):
        if i == EARLY:
            for k in range(FIRST):
                listed[base + k] = UNUSED << SEG_BIT
            first_length = base
            base = lead
        offset = (words[rows + 1, i] * CSLOT) << SEG_BIT
        for k in range(slot_count):
            listed[base + k] = words[i, k] + offset
        base = base + words[rows, i]
    for k in range(REST):
        listed[base + k] = (UNUSED << SEG_BIT) + (rows - 2) * slot_count
    return first_length, base - lead


def main_kernel(lead, words, stiffness, own, restricted_early, table, later_rows, first_row, listed, stiff, restrict, acc,
                sems):
    rows, slot_count = stiffness.shape[:2]

    def row_copy(i):
        part = pl.ds((i - EARLY) * slot_count, slot_count)
        return pltpu.make_async_copy(stiffness.at[i], stiff.at[part], sems.at[i])

    for i in range(EARLY, rows - 1):
        row_copy(i).start()
    first_length, second_length = fill_list(words, listed, rows, slot_count, lead)
    for i in range(EARLY, rows - 1):
        restrict[i] = own[i].T
    acc[...] = jnp.zeros_like(acc)

    def add(taken, restricted):
        products = [jnp.dot(y, table[column_of(w)], preferred_element_type=f32) for w, y in zip(taken, restricted)]
        for w, z in zip(taken, products):
            acc[w >> SEG_BIT] += z

    @pl.loop(0, (first_length + FIRST - 1) // FIRST)
    def _(c):
        taken = [listed[c * FIRST + u] for u in range(FIRST)]
        add(taken, [restricted_early[block_of(w)] for w in taken])

    def chunk(start, size, arrived):
        taken = [listed[lead + start + u] for u in range(size)]
        blocks = [block_of(w) for w in taken]
        needed = blocks[size - 1] // slot_count + 1

        @pl.loop(arrived, needed)
        def _(i):
            row_copy(i).wait()

        held = None
        for g in range(0, size, GROUP):
            restricted = [
                jnp.dot(restrict[b // slot_count], stiff[b - EARLY * slot_count], preferred_element_type=f32).astype(bf16)
                for b in blocks[g : g + GROUP]
            ]
            if held is not None:
                add(*held)
            held = taken[g : g + GROUP], restricted
        add(*held)
        return needed

    whole = second_length // CHUNK
    small = (second_length - whole * CHUNK + REST - 1) // REST
    arrived = lax.fori_loop(0, small, lambda c, got: chunk(c * REST, REST, got), EARLY)
    lax.fori_loop(0, whole, lambda c, got: chunk(small * REST + c * CHUNK, CHUNK, got), arrived)
    for c in range(1, NC_DEV):
        later_rows[c - 1] = acc[c * CSLOT : (c + 1) * CSLOT].astype(bf16)
    first_row[...] = acc[0:CSLOT]


def final_kernel(partial, own_part, other_part, later_rows, out, stage, sems):
    keep = lane_half() == (lax.axis_index("field") == 0)
    later = [pltpu.make_async_copy(later_rows.at[c - 1], out.at[c], sems.at[c]) for c in range(1, NC_DEV)]
    for copy in later:
        copy.start()
    copies = [pltpu.make_async_copy(stage.at[pl.ds(s, n)], out.at[0, pl.ds(s, n)], sem)
              for s, n, sem in ((0, HALF, sems.at[0]), (HALF, CSLOT - HALF, sems.at[NC_DEV]))]
    for s in range(HALF):
        mine, theirs = own_part[s].astype(f32), other_part[s].astype(f32)
        stage[s] = (partial[s] + jnp.where(keep, mine, theirs)).astype(bf16)
    copies[0].start()
    for s in range(HALF, CSLOT):
        mine, theirs = own_part[s - HALF].astype(f32), other_part[s - HALF].astype(f32)
        stage[s] = (partial[s] + pltpu.roll(jnp.where(keep, theirs, mine), 64, 1)).astype(bf16)
    copies[1].start()
    for copy in later + copies:
        copy.wait()


def shards(stiffness, prolong, columns, counts, aggregate, coarse_slots, requests):
    rows, slot_count, dofs, width = stiffness.shape
    coarse = prolong.shape[2] // dofs
    n_dom = lax.axis_size("dom")
    n_field = lax.axis_size("field")
    q = requests.shape[2]
    n_ext = rows + n_dom * q
    limit = pltpu.CompilerParams(vmem_limit_bytes=24 * 2**20)
    own_flat = prolong[:, 0, :]
    other_flat = lax.ppermute(own_flat, "field", [(0, 1), (1, 0)])
    n_words = -(-(rows + 2 + n_dom) // 8) * 8
    integers = lambda *shape: VMEM(shape, jnp.int32)
    picked, own_copy, words = pl.pallas_call(
        functools.partial(prepare_kernel, n_dom, q),
        out_shape=(VMEM(((n_dom - 1) * q, own_flat.shape[1]), bf16), VMEM(own_flat.shape, bf16),
                   integers(n_words, 128)),
        in_specs=[spec(pl.ANY)] * 6,
        out_specs=(spec(VMEM),) * 3,
        scratch_shapes=[integers(rows, slot_count), integers(rows, slot_count), integers(1, rows), integers(1, rows),
                        integers(1, n_dom, q), pltpu.SemaphoreType.DMA((6,))],
        compiler_params=limit,
    )(*map(in_hbm, (own_flat, columns, coarse_slots, counts, aggregate[None], requests)))
    g_own, g_other = [], []
    for s in range(1, n_dom):
        part = picked[(s - 1) * q : s * q]
        g_own.append(lax.ppermute(part, "dom", shift_pairs(n_dom, s)))
        pairs = [(d * n_field + f, ((d + s) % n_dom) * n_field + 1 - f) for d in range(n_dom) for f in range(n_field)]
        g_other.append(lax.ppermute(part, ("dom", "field"), pairs))
    g_own = jnp.concatenate(g_own, axis=0)
    g_other = jnp.concatenate(g_other, axis=0)
    as_blocks = lambda x: in_vmem(x.reshape(x.shape[0], dofs, coarse))
    own, other = as_blocks(own_copy), as_blocks(other_flat)
    g_own, g_other = in_vmem(g_own), in_vmem(g_other)
    block = lambda *lead: (*lead, coarse, 2 * coarse)
    words, restricted, restricted_early = pl.pallas_call(
        early_kernel,
        out_shape=(SMEM(words.shape, jnp.int32), VMEM((slot_count, coarse, width), bf16),
                   VMEM((EARLY * slot_count, coarse, width), bf16)),
        in_specs=[spec(VMEM)] * 2 + [spec(pl.ANY)],
        out_specs=(spec(SMEM), spec(VMEM), spec(VMEM)),
        scratch_shapes=[VMEM((1 + EARLY, slot_count, dofs, width), bf16), pltpu.SemaphoreType.DMA(()),
                        pltpu.SemaphoreType.DMA((1 + EARLY,))],
        compiler_params=limit,
        cost_estimate=pl.CostEstimate(flops=10**7, bytes_accessed=10**6, transcendentals=0),
    )(in_vmem(words), own, in_hbm(stiffness))
    words = pltpu.with_memory_space_constraint(words, SMEM)
    restricted, restricted_early = in_vmem(restricted), in_vmem(restricted_early)
    acc = VMEM(block(2 * HALF), f32)
    unfolding = VMEM((g_own.shape[0] * (dofs // 2 + 4), 128), f32), VMEM((dofs + 8, 128), f32)
    table, own_part = pl.pallas_call(
        functools.partial(own_spill_kernel, n_dom, q),
        out_shape=(VMEM((n_ext, width, 2 * coarse), bf16), VMEM(block(HALF), bf16)),
        in_specs=[spec(SMEM)] + [spec(VMEM)] * 3,
        out_specs=(spec(VMEM), spec(VMEM)),
        scratch_shapes=[acc, *unfolding],
        compiler_params=limit,
        cost_estimate=pl.CostEstimate(flops=10**7, bytes_accessed=10**6, transcendentals=0),
    )(words, restricted, own, g_own)
    to_next = shift_pairs(lax.axis_size("blk"), 1)
    own_part = lax.ppermute(own_part, "blk", to_next)
    table, other_part = pl.pallas_call(
        functools.partial(other_spill_kernel, n_dom, q),
        out_shape=(VMEM((n_ext, width, 2 * coarse), bf16), VMEM(block(HALF), bf16)),
        in_specs=[spec(SMEM)] + [spec(VMEM)] * 4,
        out_specs=(spec(VMEM), spec(VMEM)),
        scratch_shapes=[acc, *unfolding],
        input_output_aliases={4: 0},
        compiler_params=limit,
        cost_estimate=pl.CostEstimate(flops=10**7, bytes_accessed=10**6, transcendentals=0),
    )(words, restricted, other, g_other, in_vmem(table))
    other_part = lax.ppermute(other_part, "blk", to_next)
    out_shape = jax.ShapeDtypeStruct(block(NC_DEV, CSLOT), bf16)
    lead = EARLY * slot_count + FIRST
    later_rows, partial = pl.pallas_call(
        functools.partial(main_kernel, lead),
        out_shape=(VMEM(block(NC_DEV - 1, CSLOT), bf16), VMEM(block(CSLOT), f32)),
        in_specs=[spec(SMEM), spec(pl.ANY)] + [spec(VMEM)] * 3,
        out_specs=(spec(VMEM),) * 2,
        scratch_shapes=[SMEM((lead + rows * AVGNZ + REST + slot_count,), jnp.int32),
                        VMEM(((rows - 1 - EARLY) * slot_count, dofs, width), bf16), VMEM((rows, coarse, dofs), bf16),
                        VMEM(block(NC_DEV * CSLOT + 1), f32), pltpu.SemaphoreType.DMA((rows,))],
        compiler_params=limit,
        cost_estimate=pl.CostEstimate(flops=10**9, bytes_accessed=10**7, transcendentals=0),
    )(words, in_hbm(stiffness), own, restricted_early, in_vmem(table))
    return pl.pallas_call(
        final_kernel,
        out_shape=out_shape,
        in_specs=[spec(VMEM)] * 4,
        out_specs=spec(pl.ANY),
        scratch_shapes=[VMEM(block(CSLOT), bf16), pltpu.SemaphoreType.DMA((NC_DEV + 1,))],
        compiler_params=limit,
    )(in_vmem(partial), in_vmem(own_part), in_vmem(other_part), in_vmem(later_rows))


def solution(mesh):
    in_specs = (
        P(("dom", "blk"), None, "field", None),
        P(("dom", "blk"), "field", None),
        P(("dom", "blk"), None),
        P(("dom", "blk"), None),
        P(("dom", "blk")),
        P(("dom", "blk"), None),
        P(("dom", "blk"), None, None),
    )
    out_specs = P(("dom", "blk"), None, "field", None)
    return jax.shard_map(shards, mesh=mesh, in_specs=in_specs, out_specs=out_specs, check_vma=False)
```
